512 devices in a mesh: section: 64 (over x, y, z_lo), tp: 8 (over z_hi, core).
Axes of the slice: x: 4, y: 8, z: 8 (z_hi: 4, z_lo: 2; z = z_hi * 2 + z_lo), core: 2. Of those that a mesh axis runs over, the one named last changes fastest.
Arguments:
- queries: bfloat16 [8192, 128, 128], P('section', 'tp'), may hold values from -64 to 64
- key_heads: bfloat16 [8192, 8, 128], P('section', 'tp'), may hold values from -8 to 8
- values: bfloat16 [8192, 8, 128], P('section', 'tp'), may hold values from -6 to 6
- target: bfloat16 [8192, 128, 128], P('section', 'tp'), may hold values from -3 to 3
- map_q: float32 [128, 128, 64], P('tp'), may hold values from -1 to 1
- map_k: float32 [8, 128, 64], P('tp'), may hold values from -1 to 1
Outputs:
- grad_q: float32 [128, 128, 64], P('tp')
- grad_k: float32 [8, 128, 64], P('tp')
- distill_loss: float32 [], replicated
The draws below stay inside these ranges and needn't reach their ends.
All inputs are finite; a program needn't handle non-finite values.
Results may differ from the reference program's by a relative error of at most 0.00048.
Values may be sent and summed in bfloat16 or wider, within the bound.
No kernel may reach another device: no remote copies, remote signals or barrier semaphores. Data moves between devices by JAX's collectives and lax.ppermute only.
A program may use at most 64 MiB of HBM per device.

```python
import math
import jax
import jax.numpy as jnp
from jax import lax

HEAD_DIM = 128
GROUP = 16
FEAT = 64
WIN = 128
TOKENS = 8192
KV_HEADS = 8
HEADS = 128


def key_shared(key):
    drawn = jax.random.normal(key, (TOKENS, KV_HEADS, HEAD_DIM), jnp.float32)
    return jnp.clip(drawn, -8.0, 8.0)


def draw_key_heads(key, part):
    shared = key_shared(key)
    return shared.astype(jnp.bfloat16)


def draw_queries(key, part):
    key = jax.random.fold_in(key, 5)
    drawn = jnp.clip(jax.random.normal(key, (TOKENS, HEADS, HEAD_DIM), jnp.float32), -6.0, 6.0)
    return drawn.astype(jnp.bfloat16)


def block_levels(own_key, shape, pieces, low, largest):
    def one(position, blocks):
        heights = jax.random.uniform(jax.random.fold_in(jax.random.fold_in(own_key, 6), position), (blocks,), jnp.float32, low / len(pieces), largest / len(pieces))
        return jnp.repeat(jnp.exp(heights), shape[position] // blocks).reshape((-1,) + (1,) * (len(shape) - position - 1))

    loudness = one(*pieces[0])
    for cut in pieces[1:]:
        loudness = loudness * one(*cut)
    return loudness


def gaussian(rng, shape, scale, most, shards=(), kind=jnp.bfloat16):
    entries = scale * jax.random.normal(rng, shape, jnp.float32)
    if shards:
        entries = entries * block_levels(rng, shape, shards, -0.22, 0.18)
    return jnp.clip(entries, -most, most).astype(kind)


def setup_inputs(seed: int = 0) -> dict:
    seeds = jax.random.split(jax.random.key(seed), 7)
    queries = draw_queries(jax.random.fold_in(seeds[6], 71), 0)
    key_heads = draw_key_heads(jax.random.fold_in(seeds[6], 71), 0)
    values = gaussian(seeds[2], (TOKENS, KV_HEADS, HEAD_DIM), 1.0, 6.0, ((0, 64), (1, 8)))
    target = gaussian(seeds[3], (TOKENS, HEADS, HEAD_DIM), 0.5, 3.0, ((0, 64), (1, 8)))
    map_q = gaussian(seeds[4], (HEADS, HEAD_DIM, FEAT), 0.25, 1.0, ((0, 8),), jnp.float32)
    map_k = gaussian(seeds[5], (KV_HEADS, HEAD_DIM, FEAT), 0.25, 1.0, ((0, 8),), jnp.float32)
    return {"queries": queries, "key_heads": key_heads, "values": values, "target": target, "map_q": map_q, "map_k": map_k}


HIGH = lax.Precision.HIGHEST

def features(projected):
    both = jnp.concatenate([projected, -projected], axis=-1)
    return jax.nn.softmax(both, axis=-1)

def group_error(weight_q, weight_k, query_rows, key_rows, value_rows, target_rows):
    block_count = TOKENS // WIN
    query_float = query_rows.astype(jnp.float32)
    query_feats = features(jnp.einsum('lhd,hdf->lhf', query_float, weight_q, precision=HIGH))
    key_float = key_rows.astype(jnp.float32)
    key_feats = features(jnp.dot(key_float, weight_k, precision=HIGH))
    value_float = value_rows.astype(jnp.float32)
    key_split = key_feats.reshape(block_count, WIN, -1)
    block_s = jnp.einsum('blf,bld->bfd', key_split, value_float.reshape(block_count, WIN, HEAD_DIM), precision=HIGH)
    block_z = key_split.sum(1)
    cumul_s = jnp.cumsum(block_s, axis=0)
    cumul_z = jnp.cumsum(block_z, axis=0)
    far_state = jnp.pad(cumul_s, ((2, 0), (0, 0), (0, 0)))[:block_count]
    far_total = jnp.pad(cumul_z, ((2, 0), (0, 0)))[:block_count]
    query_blk = query_float.reshape(block_count, WIN, GROUP, HEAD_DIM)
    key_blk = key_float.reshape(block_count, WIN, HEAD_DIM)
    value_blk = value_float.reshape(block_count, WIN, HEAD_DIM)
    key_window = jnp.concatenate([jnp.pad(key_blk, ((1, 0), (0, 0), (0, 0)))[:block_count], key_blk], axis=1)
    value_window = jnp.concatenate([jnp.pad(value_blk, ((1, 0), (0, 0), (0, 0)))[:block_count], value_blk], axis=1)
    scores = jnp.einsum('bihd,bjd->bhij', query_blk, key_window, precision=HIGH) / math.sqrt(HEAD_DIM)
    row_index = jnp.arange(WIN)[:, None]
    col_index = jnp.arange(2 * WIN)[None, :]
    block_index = jnp.arange(block_count)[:, None, None]
    allowed = jnp.where(col_index < WIN, block_index > 0, col_index - WIN <= row_index)
    scores = jnp.where(allowed[:, None], scores, -1e+30)
    row_max = scores.max(-1)
    weights = jnp.exp(scores - row_max[..., None])
    window_total = weights.sum(-1)
    weights_low = lax.optimization_barrier(weights.astype(jnp.bfloat16)).astype(jnp.float32)
    window_sum = jnp.einsum('bhij,bjd->bihd', weights_low, value_window, precision=HIGH)
    feats_blk = query_feats.reshape(block_count, WIN, GROUP, -1)
    linear_sum = jnp.einsum('bihf,bfd->bihd', feats_blk, far_state, precision=HIGH)
    linear_total = jnp.einsum('bihf,bf->bih', feats_blk, far_total, precision=HIGH)
    far_scale = jnp.exp(-row_max).transpose(0, 2, 1)
    student = (window_sum + far_scale[..., None] * linear_sum) / (window_total.transpose(0, 2, 1) + far_scale * linear_total)[..., None]
    error = student - target_rows.astype(jnp.float32).reshape(block_count, WIN, GROUP, HEAD_DIM)
    return jnp.sum(error * error)

def reference(queries, key_heads, values, target, map_q, map_k):

    def per_group(group):
        query_rows = lax.dynamic_slice_in_dim(queries, group * GROUP, GROUP, 1)
        target_rows = lax.dynamic_slice_in_dim(target, group * GROUP, GROUP, 1)
        key_rows = lax.dynamic_slice_in_dim(key_heads, group, 1, 1)[:, 0]
        value_rows = lax.dynamic_slice_in_dim(values, group, 1, 1)[:, 0]
        weight_q = lax.dynamic_slice_in_dim(map_q, group * GROUP, GROUP, 0)
        weight_k = lax.dynamic_slice_in_dim(map_k, group, 1, 0)[0]
        squared, grads = jax.value_and_grad(group_error, argnums=(0, 1))(weight_q, weight_k, query_rows, key_rows, value_rows, target_rows)
        return (squared, grads[0], grads[1])
    squared, grads_q, grads_k = lax.map(per_group, jnp.arange(KV_HEADS, dtype=jnp.int32))
    count_all = float(TOKENS * HEADS * HEAD_DIM)
    grad_q = grads_q.reshape(HEADS, HEAD_DIM, FEAT) / count_all
    grad_k = grads_k / count_all
    distill_loss = jnp.sum(squared) / count_all
    return (grad_q, grad_k, distill_loss)
```

```python
import math

import jax
import jax.numpy as jnp
from jax import lax
from jax.sharding import PartitionSpec as P

WIN = 128

HIGH = lax.Precision.HIGHEST


def exchange(parts):
    return lax.all_to_all(parts, "section", 0, 0, tiled=True)


def features(projected):
    both = jnp.concatenate([projected, -projected], axis=-1)
    return jax.nn.softmax(both, axis=-1)


def pack_state(state, total, count):
    width = state.shape[-1]
    rows = state.reshape(count, -1, width)
    totals = total.reshape(count, 1, -1)
    totals = jnp.pad(totals, ((0, 0), (0, 0), (0, width - totals.shape[-1])))
    return jnp.concatenate([rows, totals], axis=1)


def unpack_state(parts, feats, width):
    count = parts.shape[0]
    per = feats // count
    state = parts[:, :per].reshape(feats, width)
    total = parts[:, per, :per].reshape(feats)
    return state, total


def on_device(queries, key_heads, values, target, map_q, map_k):
    tokens, head_count, width = queries.shape
    count = lax.axis_size("section")
    position = lax.axis_index("section")
    has_prev = position > 0
    tp_count = lax.axis_size("tp")
    count_all = float(tokens * head_count * width * count * tp_count)
    key_rows = key_heads[:, 0, :]
    value_rows = values[:, 0, :]
    halo = lax.ppermute(
        jnp.concatenate([key_rows, value_rows], axis=0),
        "section",
        [(i, i + 1) for i in range(count - 1)],
    )
    halo_keys, halo_values = halo[:tokens], halo[tokens:]
    value_float = value_rows.astype(jnp.float32)
    feats = 2 * map_q.shape[-1]

    def block_state(weight_k):
        feats_k = features(jnp.dot(key_rows.astype(jnp.float32), weight_k[0], precision=HIGH))
        return jnp.dot(feats_k.T, value_float, precision=HIGH), feats_k.sum(0)

    (own_s, own_z), state_back = jax.vjp(block_state, map_k)
    index = jnp.arange(count)
    before = (index[None, :] + 2 <= index[:, None]).astype(jnp.float32)

    gathered = exchange(pack_state(own_s, own_z, count))
    prefix = jnp.dot(before, gathered.reshape(count, -1), precision=HIGH)
    far_s, far_z = unpack_state(exchange(prefix.reshape(gathered.shape)), feats, width)

    def student_error(weight_q, far_state, far_total):
        query_feats = features(
            jnp.einsum("thd,hdf->htf", queries.astype(jnp.float32), weight_q, precision=HIGH)
        )
        key_window = jnp.concatenate([halo_keys, key_rows], axis=0)
        value_window = jnp.concatenate([halo_values, value_rows], axis=0)
        scores = jnp.einsum(
            "ihd,jd->hij", queries, key_window, preferred_element_type=jnp.float32
        ) / math.sqrt(width)
        row_index = jnp.arange(WIN)[:, None]
        col_index = jnp.arange(2 * WIN)[None, :]
        allowed = jnp.where(col_index < WIN, has_prev, col_index - WIN <= row_index)
        scores = jnp.where(allowed[None], scores, -1e30)
        row_max = scores.max(-1)
        weights = jnp.exp(scores - row_max[..., None])
        window_total = weights.sum(-1)
        window_sum = jnp.einsum(
            "hij,jd->hid",
            weights.astype(jnp.bfloat16),
            value_window,
            preferred_element_type=jnp.float32,
        )
        linear_sum = jnp.einsum("hif,fd->hid", query_feats, far_state, precision=HIGH)
        linear_total = jnp.einsum("hif,f->hi", query_feats, far_total, precision=HIGH)
        far_scale = jnp.exp(-row_max)
        student = (window_sum + far_scale[..., None] * linear_sum) / (
            window_total + far_scale * linear_total
        )[..., None]
        error = student - target.astype(jnp.float32).transpose(1, 0, 2)
        return jnp.sum(error * error) / count_all

    loss_local, (grad_q, grad_s, grad_z) = jax.value_and_grad(student_error, argnums=(0, 1, 2))(
        map_q, far_s, far_z
    )

    packed = pack_state(grad_s, grad_z, count)
    state_rows = packed.shape[1]
    packed = packed.at[:, -1, -1].set(loss_local)
    query_parts = grad_q.reshape(count, -1, width)
    parts = exchange(jnp.concatenate([packed, query_parts], axis=1))
    state_parts = parts[:, :state_rows]
    loss = state_parts[:, -1, -1].sum()
    suffix = jnp.dot(before.T, state_parts.reshape(count, -1), precision=HIGH)
    query_sum = parts[:, state_rows:].sum(0)
    back = exchange(
        jnp.concatenate(
            [
                suffix.reshape(state_parts.shape),
                jnp.broadcast_to(query_sum[None], (count,) + query_sum.shape),
            ],
            axis=1,
        )
    )
    later_s, later_z = unpack_state(back[:, :state_rows], feats, width)
    (grad_k,) = state_back((later_s, later_z))
    key_sum = exchange(grad_k.reshape(count, 1, -1)).sum(0)
    grad_k = exchange(jnp.broadcast_to(key_sum[None], (count,) + key_sum.shape))
    for bit in (1, 2, 4):
        loss = loss + lax.ppermute(loss, "tp", [(i, i ^ bit) for i in range(tp_count)])
    return back[:, state_rows:].reshape(map_q.shape), grad_k.reshape(map_k.shape), loss


def solution(mesh):
    in_specs = (
        P("section", "tp", None),
        P("section", "tp", None),
        P("section", "tp", None),
        P("section", "tp", None),
        P("tp", None, None),
        P("tp", None, None),
    )
    out_specs = (P("tp", None, None), P("tp", None, None), P())
    return jax.shard_map(
        on_device, mesh=mesh, in_specs=in_specs, out_specs=out_specs, check_vma=False
    )
```

```python
import math

import jax
import jax.numpy as jnp
from jax import lax
from jax.sharding import PartitionSpec as P

WIN = 128

HIGH = lax.Precision.HIGHEST


def exchange(parts, axis="section"):
    return lax.all_to_all(parts, axis, 0, 0, tiled=True)


def spread(part, count):
    return jnp.broadcast_to(part[None], (count,) + part.shape)


def features(projected):
    both = jnp.concatenate([projected, -projected], axis=-1)
    return jax.nn.softmax(both, axis=-1)


def features_back(feats, grad):
    half = feats.shape[-1] // 2
    inner = feats * (grad - (feats * grad).sum(-1, keepdims=True))
    return inner[..., :half] - inner[..., half:]


def pack_state(state, total, count):
    width = state.shape[-1]
    rows = state.reshape(count, -1, width)
    totals = total.reshape(count, 1, -1)
    totals = jnp.pad(totals, ((0, 0), (0, 0), (0, width - totals.shape[-1])))
    return jnp.concatenate([rows, totals], axis=1)


def unpack_state(parts, feats, width):
    per = feats // parts.shape[0]
    state = parts[:, :per].reshape(feats, width)
    total = parts[:, per, :per].reshape(feats)
    return state, total


def on_device(queries, key_heads, values, target, map_q, map_k):
    tokens, head_count, width = queries.shape
    count = lax.axis_size("section")
    position = lax.axis_index("section")
    tp_count = lax.axis_size("tp")
    count_all = float(tokens * head_count * width * count * tp_count)
    key_rows = key_heads[:, 0, :]
    value_rows = values[:, 0, :]
    key_float = key_rows.astype(jnp.float32)
    value_float = value_rows.astype(jnp.float32)
    feats = 2 * map_q.shape[-1]
    index = jnp.arange(count)
    before = (index[None, :] + 2 <= index[:, None]).astype(jnp.float32)

    with jax.named_scope("own_state"):
        key_feats = features(jnp.dot(key_float, map_k[0], precision=HIGH))
        own_s = jnp.dot(key_feats.T, value_float, precision=HIGH)
        packed = pack_state(own_s, key_feats.sum(0), count)
    with jax.named_scope("states_out"):
        gathered = exchange(packed)
    halo = lax.ppermute(
        jnp.concatenate([key_rows, value_rows], axis=0),
        "section",
        [(i, i + 1) for i in range(count - 1)],
    )
    with jax.named_scope("query_feats"):
        query_heads = queries.transpose(1, 0, 2)
        query_feats = features(
            jnp.einsum("htd,hdf->htf", query_heads.astype(jnp.float32), map_q, precision=HIGH)
        )
        target_float = target.transpose(1, 0, 2).astype(jnp.float32)
    with jax.named_scope("prefix"):
        prefix = jnp.dot(before, gathered.reshape(count, -1), precision=HIGH)
        prefix, halo, query_feats, target_float = lax.optimization_barrier(
            (prefix, halo, query_feats, target_float)
        )
    with jax.named_scope("states_back"):
        returned = exchange(prefix.reshape(packed.shape))

    with jax.named_scope("window"):
        key_window = jnp.concatenate([halo[:tokens], key_rows], axis=0)
        value_window = jnp.concatenate([halo[tokens:], value_rows], axis=0)
        scores = jnp.einsum(
            "hid,jd->hij", query_heads, key_window, preferred_element_type=jnp.float32
        ) / math.sqrt(width)
        row_index = jnp.arange(WIN)[:, None]
        col_index = jnp.arange(2 * WIN)[None, :]
        allowed = jnp.where(col_index < WIN, position > 0, col_index - WIN <= row_index)
        scores = jnp.where(allowed[None], scores, -1e30)
        row_max = scores.max(-1)
        weights = jnp.exp(scores - row_max[..., None])
        window_total = weights.sum(-1)
        window_sum = jnp.einsum(
            "hij,jd->hid",
            weights.astype(jnp.bfloat16),
            value_window,
            preferred_element_type=jnp.float32,
        )
        far_scale = jnp.exp(-row_max)
        returned, window_sum, window_total, far_scale = lax.optimization_barrier(
            (returned, window_sum, window_total, far_scale)
        )

    with jax.named_scope("student"):
        far_state, far_total = unpack_state(returned, feats, width)
        linear_sum = jnp.einsum("hif,fd->hid", query_feats, far_state, precision=HIGH)
        linear_total = jnp.einsum("hif,f->hi", query_feats, far_total, precision=HIGH)
        divisor = window_total + far_scale * linear_total
        student = (window_sum + far_scale[..., None] * linear_sum) / divisor[..., None]
        error = student - target_float
        loss_local = jnp.sum(error * error) / count_all
        scale = far_scale * (2.0 / count_all) / divisor
        grad_sum = error * scale[..., None]
        grad_total = -(grad_sum * student).sum(-1)
        grad_s = jnp.einsum("hif,hid->fd", query_feats, grad_sum, precision=HIGH)
        grad_z = jnp.einsum("hif,hi->f", query_feats, grad_total, precision=HIGH)
        packed = pack_state(grad_s, grad_z, count)
    with jax.named_scope("grads_out"):
        gathered = exchange(packed)
    with jax.named_scope("loss_tp"):
        loss_tp = loss_local
        for bit in (1, 2, 4):
            other = lax.ppermute(loss_tp, "tp", [(i, i ^ bit) for i in range(tp_count)])
            loss_tp = loss_tp + other
        loss_rows = jnp.broadcast_to(loss_tp, (count, 1, width))

    with jax.named_scope("grad_q"):
        grad_feats = (
            jnp.einsum("hid,fd->hif", grad_sum, far_state, precision=HIGH)
            + grad_total[..., None] * far_total
        )
        grad_proj = features_back(query_feats, grad_feats)
        grad_q = jnp.einsum(
            "htd,htf->hfd", query_heads.astype(jnp.float32), grad_proj, precision=HIGH
        )
    with jax.named_scope("suffix"):
        suffix = jnp.dot(before.T, gathered.reshape(count, -1), precision=HIGH)
    with jax.named_scope("grads_back"):
        later_s, later_z = unpack_state(exchange(suffix.reshape(packed.shape)), feats, width)
    with jax.named_scope("grad_k"):
        grad_feats = jnp.dot(value_float, later_s.T, precision=HIGH) + later_z
        grad_k = jnp.dot(features_back(key_feats, grad_feats).T, key_float, precision=HIGH)
    with jax.named_scope("maps_out"):
        parts = jnp.concatenate(
            [grad_q.reshape(count, -1, width), grad_k.reshape(count, 1, -1), loss_rows], axis=1
        )
        sums = exchange(parts).sum(0)
        loss = sums[-1, 0]
    with jax.named_scope("maps_back"):
        maps = exchange(spread(sums[:-1], count))
        grad_q = maps[:, :-1].reshape(head_count, -1, width).transpose(0, 2, 1)
        grad_k = maps[:, -1].reshape(-1, width).T
    return grad_q, grad_k[None], loss


def solution(mesh):
    in_specs = (
        P("section", "tp", None),
        P("section", "tp", None),
        P("section", "tp", None),
        P("section", "tp", None),
        P("tp", None, None),
        P("tp", None, None),
    )
    out_specs = (P("tp", None, None), P("tp", None, None), P())
    return jax.shard_map(
        on_device, mesh=mesh, in_specs=in_specs, out_specs=out_specs, check_vma=False
    )
```

```python
import math

import jax
import jax.numpy as jnp
from jax import lax
from jax.experimental import pallas as pl
from jax.experimental.pallas import tpu as pltpu
from jax.sharding import PartitionSpec as P

NN = (((1,), (0,)), ((), ()))
NT = (((1,), (1,)), ((), ()))
LIMIT = 40 * 1024 * 1024
STEPS = 4
PAIR = 256


def exchange(parts, axis="section"):
    return lax.all_to_all(parts, axis, 0, 0, tiled=True)


def mxu(a, b, dims=NN):
    return lax.dot_general(a, b, dims, preferred_element_type=jnp.float32)


def split(x, terms=2):
    out = []
    for _ in range(terms - 1):
        high = x.astype(jnp.bfloat16)
        out.append(high)
        x = x - high.astype(jnp.float32)
    out.append(x.astype(jnp.bfloat16))
    return out


def mxu3(a, b, dims=NN):
    return mxu(a[0], b[0], dims) + (mxu(a[0], b[1], dims) + mxu(a[1], b[0], dims))


def features_t(weight, rows):
    both = jnp.concatenate([weight, -weight], axis=0)
    proj = sum(mxu(term, rows, NT) for term in reversed(split(both, 3)))
    half = proj.shape[0] // 2
    top = jnp.max(jnp.abs(proj[:half]), axis=0, keepdims=True)
    raised = jnp.exp(proj - top)
    return raised * (1.0 / jnp.sum(raised, axis=0, keepdims=True))


def features_back_t(feats, grad):
    return feats * (grad - jnp.sum(feats * grad, axis=0, keepdims=True))


def put_state(ref, state, total):
    half = state.shape[0] // 2
    lane = lax.broadcasted_iota(jnp.int32, (half, state.shape[1]), 1)
    ref[:, 0, :] = state[:half]
    ref[:, 1, :] = state[half:]
    ref[:, 2, :] = jnp.where(lane < half, total[:half], total[half:])


def get_state(ref):
    state = jnp.concatenate([ref[:, 0, :], ref[:, 1, :]], axis=0)
    totals = ref[:, 2, :]
    half, width = totals.shape
    total = jnp.concatenate(
        [
            jnp.broadcast_to(totals[:, :1], (half, width)),
            jnp.broadcast_to(totals[:, half : half + 1], (half, width)),
        ],
        axis=0,
    )
    return state, total


def key_kernel(key_ref, value_ref, map_ref, parts_ref, feats_ref):
    feats = features_t(map_ref[0], key_ref[...])
    feats_ref[...] = feats
    state = sum(mxu(term, value_ref[...]) for term in reversed(split(feats)))
    total = jnp.broadcast_to(jnp.sum(feats, axis=1, keepdims=True), state.shape)
    put_state(parts_ref, state, total)


def running_kernel(backward, parts_ref, out_ref):
    count = parts_ref.shape[0]
    row = lax.broadcasted_iota(jnp.int32, (count, count), 0)
    col = lax.broadcasted_iota(jnp.int32, (count, count), 1)
    wanted = (row + 2 <= col) if backward else (col + 2 <= row)
    chosen = jnp.where(wanted, 1.0, 0.0).astype(jnp.bfloat16)
    for k in range(parts_ref.shape[1]):
        terms = split(parts_ref[:, k, :], 3)
        out_ref[:, k, :] = sum(mxu(chosen, term) for term in reversed(terms))


def query_kernel(query_ref, map_ref, high_ref, low_ref):
    tokens = query_ref.shape[0] // map_ref.shape[0]
    for h in range(map_ref.shape[0]):
        here = slice(h * tokens, (h + 1) * tokens)
        high_ref[:, here], low_ref[:, here] = split(features_t(map_ref[h], query_ref[here, :]))


def window_kernel(
    query_ref, key_ref, value_ref, halo_ref, target_ref, sum_ref, scale_ref, target_t_ref
):
    tokens, width = key_ref.shape
    has_prev = lax.axis_index("section") > 0
    row = lax.broadcasted_iota(jnp.int32, (tokens, PAIR), 0)
    col = lax.broadcasted_iota(jnp.int32, (tokens, PAIR), 1)
    earlier = row <= lax.rem(col, tokens)
    root = 1.0 / math.sqrt(width)
    halo_keys = halo_ref[:tokens]
    halo_values_t = halo_ref[tokens:].astype(jnp.float32).T.astype(jnp.bfloat16)
    values_t = value_ref[...].astype(jnp.float32).T.astype(jnp.bfloat16)
    for k in range(query_ref.shape[0] // PAIR):
        here = slice(k * PAIR, (k + 1) * PAIR)
        query = query_ref[here, :]
        before = jnp.where(has_prev, mxu(halo_keys, query, NT) * root, -1e30)
        own = jnp.where(earlier, mxu(key_ref[...], query, NT) * root, -1e30)
        top = jnp.max(jnp.maximum(before, own), axis=0, keepdims=True)
        before = jnp.exp(before - top)
        own = jnp.exp(own - top)
        inverse = 1.0 / jnp.sum(before + own, axis=0, keepdims=True)
        total = mxu(halo_values_t, before.astype(jnp.bfloat16)) + mxu(
            values_t, own.astype(jnp.bfloat16)
        )
        sum_ref[:, here] = total * inverse
        scale_ref[:, here] = jnp.exp(-top) * inverse
        target_t_ref[:, here] = target_ref[here, :].astype(jnp.float32).T.astype(jnp.bfloat16)


def student_kernel(
    factor,
    high_ref,
    low_ref,
    sum_ref,
    scale_ref,
    target_ref,
    state_ref,
    parts_ref,
    loss_ref,
    grad_high_ref,
    grad_low_ref,
    grad_total_ref,
    state_high,
    state_low,
    total_acc,
    grad_acc,
    grad_total_acc,
    loss_acc,
):
    step = pl.program_id(0)

    @pl.when(step == 0)
    def _():
        state, total = get_state(state_ref)
        state_high[...], state_low[...] = split(state.T)
        total_acc[...] = total
        grad_acc[...] = jnp.zeros_like(grad_acc)
        grad_total_acc[...] = jnp.zeros_like(grad_total_acc)
        loss_acc[...] = jnp.zeros_like(loss_acc)

    state = (state_high[...], state_low[...])
    total = jnp.concatenate([total_acc[...]] * (PAIR // total_acc.shape[1]), axis=1)
    for k in range(sum_ref.shape[1] // PAIR):
        here = slice(k * PAIR, (k + 1) * PAIR)
        pair = (high_ref[:, here], low_ref[:, here])
        feats = pair[0].astype(jnp.float32) + pair[1].astype(jnp.float32)
        scale = scale_ref[:, here]
        linear_total = jnp.sum(feats * total, axis=0, keepdims=True)
        inverse = 1.0 / (1.0 + scale * linear_total)
        student = (sum_ref[:, here] + scale * mxu3(state, pair)) * inverse
        error = student - target_ref[:, here].astype(jnp.float32)
        loss_acc[...] += error * error
        grad_sum = error * (scale * inverse * factor)
        grad_total = -jnp.sum(grad_sum * student, axis=0, keepdims=True)
        grads = split(grad_sum)
        grad_high_ref[:, here], grad_low_ref[:, here] = grads
        grad_total_ref[:, here] = grad_total
        grad_acc[...] += mxu3(pair, grads, NT)
        grad_total_acc[...] += feats * grad_total

    @pl.when(step == pl.num_programs(0) - 1)
    def _():
        grad = grad_acc[...]
        grad_total = jnp.sum(grad_total_acc[...], axis=1, keepdims=True)
        put_state(parts_ref, grad, jnp.broadcast_to(grad_total, grad.shape))
        loss_ref[...] = jnp.full(loss_ref.shape, jnp.sum(loss_acc[...]) * (0.5 * factor))


def grad_q_kernel(
    high_ref, low_ref, grad_high_ref, grad_low_ref, grad_total_ref, query_ref, state_ref, out_ref
):
    state, total = get_state(state_ref)
    total = jnp.concatenate([total] * (PAIR // total.shape[1]), axis=1)
    state = split(state)
    heads, half, _ = out_ref.shape
    tokens = query_ref.shape[0] // heads
    for k in range(query_ref.shape[0] // PAIR):
        here = slice(k * PAIR, (k + 1) * PAIR)
        grad = mxu3(state, (grad_high_ref[:, here], grad_low_ref[:, here]))
        grad = grad + total * grad_total_ref[:, here]
        feats = high_ref[:, here].astype(jnp.float32) + low_ref[:, here].astype(jnp.float32)
        inner = split(features_back_t(feats, grad))
        for n in range(PAIR // tokens):
            cut = slice(n * tokens, (n + 1) * tokens)
            query = query_ref[k * PAIR + n * tokens : k * PAIR + (n + 1) * tokens, :]
            out = mxu(inner[1][:, cut], query) + mxu(inner[0][:, cut], query)
            out_ref[k * (PAIR // tokens) + n] = out[:half] - out[half:]


def grad_k_kernel(state_ref, feats_ref, key_ref, value_ref, query_ref, out_ref):
    state, total = get_state(state_ref)
    grad = sum(mxu(term, value_ref[...], NT) for term in reversed(split(state))) + total
    inner = split(features_back_t(feats_ref[...], grad))
    out = mxu(inner[1], key_ref[...]) + mxu(inner[0], key_ref[...])
    half = out.shape[0] // 2
    heads = query_ref.shape[0]
    for h in range(heads):
        out_ref[:, h // 2, h % 2, :] = query_ref[h]
    out_ref[:, heads // 2, 0, :] = out[:half] - out[half:]
    out_ref[:, heads // 2, 1, :] = jnp.zeros((half, out.shape[1]), jnp.float32)


def total_kernel(parts_ref, loss_ref, out_ref):
    total = jnp.sum(parts_ref[...], axis=0)
    out_ref[...] = jnp.broadcast_to(total[None], out_ref.shape)
    count, last, _, width = out_ref.shape
    out_ref[:, last - 1, 1, :] = jnp.broadcast_to(loss_ref[:1], (count, width))


def finish_kernel(parts_ref, query_ref, key_ref, loss_ref):
    heads = query_ref.shape[0]
    for h in range(heads):
        query_ref[h] = parts_ref[:, h // 2, h % 2, :]
    key_ref[...] = parts_ref[:, heads // 2, 0, :]
    loss_ref[...] = jnp.sum(parts_ref[:, heads // 2, 1, :], axis=0, keepdims=True)


def call(kernel, out_shape, cost, grid=None, in_specs=None, out_specs=None, scratch=()):
    extra = {} if grid is None else dict(grid=grid, in_specs=in_specs, out_specs=out_specs)
    flops, nbytes = cost
    return pl.pallas_call(
        kernel,
        out_shape=out_shape,
        scratch_shapes=scratch,
        compiler_params=pltpu.CompilerParams(vmem_limit_bytes=LIMIT),
        cost_estimate=pl.CostEstimate(flops=flops, bytes_accessed=nbytes, transcendentals=0),
        **extra,
    )


def shape(*dims, dtype=jnp.float32):
    return jax.ShapeDtypeStruct(dims, dtype)


def far(*dims, dtype=jnp.float32):
    return pltpu.HBM(dims, dtype)


def keep_far(*arrays):
    return [pltpu.with_memory_space_constraint(array, pltpu.HBM) for array in arrays]


def whole(*dims):
    return pl.BlockSpec(dims, lambda i: (0,) * len(dims))


def on_device(queries, key_heads, values, target, map_q, map_k):
    tokens, heads, width = queries.shape
    count = lax.axis_size("section")
    tp_count = lax.axis_size("tp")
    count_all = float(tokens * heads * width * count * tp_count)
    key_rows = key_heads[:, 0, :]
    value_rows = values[:, 0, :]
    map_q = map_q.transpose(0, 2, 1)
    map_k = map_k.transpose(0, 2, 1)
    half = map_q.shape[1]
    feats = 2 * half
    per = heads // STEPS
    positions = heads * tokens
    low = jnp.bfloat16
    mega = 1 << 20
    by_row = pl.BlockSpec((positions // STEPS, width), lambda i: (i, 0))
    by_head = pl.BlockSpec((per, half, width), lambda i: (i, 0, 0))

    def by_lane(rows):
        return pl.BlockSpec((rows, positions // STEPS), lambda i: (0, i))

    parts_shape = shape(count, 3, width)
    with jax.named_scope("own_state"):
        packed, key_feats = call(
            key_kernel, (parts_shape, shape(feats, tokens)), (30 * mega, mega // 2)
        )(*keep_far(key_rows, value_rows, map_k))
    with jax.named_scope("states_out"):
        gathered = exchange(packed)
    halo_keys, halo_values, key_feats = lax.optimization_barrier((key_rows, value_rows, key_feats))
    halo = lax.ppermute(
        jnp.concatenate([halo_keys, halo_values], axis=0),
        "section",
        [(i, i + 1) for i in range(count - 1)],
    )
    with jax.named_scope("query_feats"):
        query_rows = queries.transpose(1, 0, 2).reshape(positions, width)
        target_rows = target.transpose(1, 0, 2).reshape(positions, width)
        pair_shape = far(feats, positions, dtype=low)
        pair = call(
            query_kernel,
            (pair_shape, pair_shape),
            (600 * mega, 3 * mega),
            (STEPS,),
            [by_row, by_head],
            [by_lane(feats)] * 2,
        )(query_rows, map_q)
    with jax.named_scope("prefix"):
        prefix = call(lambda *refs: running_kernel(False, *refs), parts_shape, (mega, mega // 4))(
            gathered
        )
        prefix, halo, query_rows, target_rows, pair = lax.optimization_barrier(
            (prefix, halo, query_rows, target_rows, pair)
        )
    with jax.named_scope("states_back"):
        returned = exchange(prefix)
    with jax.named_scope("window"):
        window = call(
            window_kernel,
            (far(width, positions), far(1, positions), far(width, positions, dtype=low)),
            (2000 * mega, 8 * mega),
            (STEPS,),
            [by_row, whole(tokens, width), whole(tokens, width), whole(2 * tokens, width), by_row],
            [by_lane(width), by_lane(1), by_lane(width)],
        )(query_rows, key_rows, value_rows, halo, target_rows)
    with jax.named_scope("student"):
        grad_shape = far(width, positions, dtype=low)
        packed, loss_local, *grads = call(
            lambda *refs: student_kernel(2.0 / count_all, *refs),
            (parts_shape, shape(8, width), grad_shape, grad_shape, far(1, positions)),
            (400 * mega, 4 * mega),
            (STEPS,),
            [by_lane(feats), by_lane(feats), by_lane(width), by_lane(1), by_lane(width)]
            + [whole(count, 3, width)],
            [whole(count, 3, width), whole(8, width)]
            + [by_lane(width), by_lane(width), by_lane(1)],
            [
                pltpu.VMEM((width, feats), low),
                pltpu.VMEM((width, feats), low),
                pltpu.VMEM((feats, width), jnp.float32),
                pltpu.VMEM((feats, width), jnp.float32),
                pltpu.VMEM((feats, PAIR), jnp.float32),
                pltpu.VMEM((width, PAIR), jnp.float32),
            ],
        )(*keep_far(*pair, *window), returned)
    with jax.named_scope("grads_out"):
        gathered = exchange(packed)
    with jax.named_scope("grad_q"):
        grad_q = call(
            grad_q_kernel,
            shape(heads, half, width),
            (1000 * mega, 4 * mega),
            (STEPS,),
            [by_lane(feats), by_lane(feats), by_lane(width), by_lane(width), by_lane(1)]
            + [by_row, whole(count, 3, width)],
            by_head,
        )(*keep_far(*pair, *grads, query_rows), returned)
    with jax.named_scope("suffix"):
        suffix = call(lambda *refs: running_kernel(True, *refs), parts_shape, (mega, mega // 4))(
            gathered
        )
    with jax.named_scope("grads_back"):
        later = exchange(suffix)

    def over_tp(loss, bit):
        return loss + lax.ppermute(loss, "tp", [(i, i ^ bit) for i in range(tp_count)])

    with jax.named_scope("loss_near"):
        loss = over_tp(loss_local, 1)
    maps_shape = shape(count, heads // 2 + 1, 2, width)

    def exchange_maps(parts):
        return exchange(parts.reshape(-1, 2, width)).reshape(parts.shape)

    with jax.named_scope("grad_k"):
        parts = call(grad_k_kernel, maps_shape, (20 * mega, mega))(
            later, key_feats, key_rows, value_rows, grad_q
        )
        parts, loss = lax.optimization_barrier((parts, loss))
    with jax.named_scope("loss_far"):
        loss = over_tp(over_tp(loss, 2), 4)
    with jax.named_scope("maps_out"):
        sums = call(total_kernel, maps_shape, (mega, mega))(exchange_maps(parts), loss)
    with jax.named_scope("maps_back"):
        grad_q, grad_k, loss = call(
            finish_kernel,
            (shape(heads, half, width), shape(half, width), shape(1, width)),
            (mega, mega),
        )(exchange_maps(sums))
        grad_q = grad_q.transpose(0, 2, 1)
        grad_k = grad_k.T
        loss = loss[0, 0]
    return grad_q, grad_k[None], loss


def solution(mesh):
    in_specs = (
        P("section", "tp", None),
        P("section", "tp", None),
        P("section", "tp", None),
        P("section", "tp", None),
        P("tp", None, None),
        P("tp", None, None),
    )
    out_specs = (P("tp", None, None), P("tp", None, None), P())
    return jax.shard_map(
        on_device, mesh=mesh, in_specs=in_specs, out_specs=out_specs, check_vma=False
    )
```

```python
import math

import jax
import jax.numpy as jnp
from jax import lax
from jax.experimental import pallas as pl
from jax.experimental.pallas import tpu as pltpu
from jax.sharding import PartitionSpec as P

NN = (((1,), (0,)), ((), ()))
NT = (((1,), (1,)), ((), ()))
LIMIT = 40 * 1024 * 1024
STEPS = 4
PAIR = 256
SUBLANES = 8


def exchange(parts, axis="section"):
    return lax.all_to_all(parts, axis, 0, 0, tiled=True)


def mxu(a, b, dims=NN):
    return lax.dot_general(a, b, dims, preferred_element_type=jnp.float32)


def split(x, terms=2):
    out = []
    for _ in range(terms - 1):
        high = x.astype(jnp.bfloat16)
        out.append(high)
        x = x - high.astype(jnp.float32)
    out.append(x.astype(jnp.bfloat16))
    return out


def mxu3(a, b, dims=NN):
    return mxu(a[0], b[0], dims) + (mxu(a[0], b[1], dims) + mxu(a[1], b[0], dims))


def features_t(weight, rows):
    both = jnp.concatenate([weight, -weight], axis=0)
    proj = sum(mxu(term, rows, NT) for term in reversed(split(both, 3)))
    half = proj.shape[0] // 2
    top = jnp.max(jnp.abs(proj[:half]), axis=0, keepdims=True)
    raised = jnp.exp(proj - top)
    return raised * (1.0 / jnp.sum(raised, axis=0, keepdims=True))


def features_back_t(feats, grad):
    return feats * (grad - jnp.sum(feats * grad, axis=0, keepdims=True))


def put_state(ref, state, total):
    half = state.shape[0] // 2
    lane = lax.broadcasted_iota(jnp.int32, (half, state.shape[1]), 1)
    ref[:, 0, :] = state[:half]
    ref[:, 1, :] = state[half:]
    ref[:, 2, :] = jnp.where(lane < half, total[:half], total[half:])


def get_state(ref):
    state = jnp.concatenate([ref[:, 0, :], ref[:, 1, :]], axis=0)
    totals = ref[:, 2, :]
    half, width = totals.shape
    total = jnp.concatenate(
        [
            jnp.broadcast_to(totals[:, :1], (half, width)),
            jnp.broadcast_to(totals[:, half : half + 1], (half, width)),
        ],
        axis=0,
    )
    return state, total


def key_kernel(key_ref, value_ref, map_ref, parts_ref, feats_ref):
    feats = features_t(map_ref[0], key_ref[...])
    feats_ref[...] = feats
    state = sum(mxu(term, value_ref[...]) for term in reversed(split(feats)))
    total = jnp.broadcast_to(jnp.sum(feats, axis=1, keepdims=True), state.shape)
    put_state(parts_ref, state, total)


def running_kernel(backward, parts_ref, out_ref, *loss_ref):
    count = parts_ref.shape[0]
    row = lax.broadcasted_iota(jnp.int32, (count, count), 0)
    col = lax.broadcasted_iota(jnp.int32, (count, count), 1)
    wanted = (row + 2 <= col) if backward else (col + 2 <= row)
    chosen = jnp.where(wanted, 1.0, 0.0).astype(jnp.bfloat16)
    for k in range(parts_ref.shape[1]):
        terms = split(parts_ref[:, k, :], 3)
        out_ref[:, k, :] = sum(mxu(chosen, term) for term in reversed(terms))
    if loss_ref:
        width = parts_ref.shape[2]
        loss = jnp.sum(parts_ref[:, 2, width - 1 :], axis=0, keepdims=True)
        loss_ref[0][...] = jnp.broadcast_to(loss, loss_ref[0].shape)


def query_kernel(query_ref, map_ref, high_ref, low_ref):
    tokens = query_ref.shape[0] // map_ref.shape[0]
    for h in range(map_ref.shape[0]):
        here = slice(h * tokens, (h + 1) * tokens)
        high_ref[:, here], low_ref[:, here] = split(features_t(map_ref[h], query_ref[here, :]))


def window_kernel(
    query_ref, key_ref, value_ref, halo_ref, target_ref, sum_ref, scale_ref, target_t_ref
):
    tokens, width = key_ref.shape
    has_prev = lax.axis_index("section") > 0
    row = lax.broadcasted_iota(jnp.int32, (tokens, PAIR), 0)
    col = lax.broadcasted_iota(jnp.int32, (tokens, PAIR), 1)
    earlier = row <= lax.rem(col, tokens)
    root = 1.0 / math.sqrt(width)
    halo_keys = halo_ref[:tokens]
    halo_values_t = halo_ref[tokens:].astype(jnp.float32).T.astype(jnp.bfloat16)
    values_t = value_ref[...].astype(jnp.float32).T.astype(jnp.bfloat16)
    for k in range(query_ref.shape[0] // PAIR):
        here = slice(k * PAIR, (k + 1) * PAIR)
        query = query_ref[here, :]
        before = jnp.where(has_prev, mxu(halo_keys, query, NT) * root, -1e30)
        own = jnp.where(earlier, mxu(key_ref[...], query, NT) * root, -1e30)
        top = jnp.max(jnp.maximum(before, own), axis=0, keepdims=True)
        before = jnp.exp(before - top)
        own = jnp.exp(own - top)
        inverse = 1.0 / jnp.sum(before + own, axis=0, keepdims=True)
        total = mxu(halo_values_t, before.astype(jnp.bfloat16)) + mxu(
            values_t, own.astype(jnp.bfloat16)
        )
        sum_ref[:, here] = total * inverse
        scale_ref[:, here] = jnp.exp(-top) * inverse
        target_t_ref[:, here] = target_ref[here, :].astype(jnp.float32).T.astype(jnp.bfloat16)


def student_kernel(
    factor,
    high_ref,
    low_ref,
    sum_ref,
    scale_ref,
    target_ref,
    state_ref,
    parts_ref,
    grad_high_ref,
    grad_low_ref,
    grad_total_ref,
):
    state, total = get_state(state_ref)
    width = state.shape[1]
    extra = 2 * SUBLANES
    state = split(jnp.concatenate([state.T, total.T[:extra]], axis=0))
    grad_both = 0.0
    loss = 0.0
    for k in range(sum_ref.shape[1] // PAIR):
        here = slice(k * PAIR, (k + 1) * PAIR)
        pair = (high_ref[:, here], low_ref[:, here])
        scale = scale_ref[:, here]
        linear = mxu3(state, pair)
        inverse = 1.0 / (1.0 + scale * linear[width : width + 1])
        student = (sum_ref[:, here] + scale * linear[:width]) * inverse
        error = student - target_ref[:, here].astype(jnp.float32)
        loss = loss + jnp.sum((error * error).reshape(-1, SUBLANES, PAIR), axis=0)
        grad_sum = error * (scale * inverse * factor)
        grad_total = -jnp.sum(grad_sum * student, axis=0, keepdims=True)
        grads = split(grad_sum)
        grad_high_ref[:, here], grad_low_ref[:, here] = grads
        grad_total_ref[:, here] = grad_total
        totals = split(jnp.broadcast_to(grad_total, (extra, PAIR)))
        grads = [jnp.concatenate(both, axis=0) for both in zip(grads, totals)]
        grad_both = grad_both + mxu3(pair, grads, NT)
    grad = grad_both[:, :width]
    total = jnp.broadcast_to(grad_both[:, width : width + 1], grad.shape)
    lane = lax.broadcasted_iota(jnp.int32, total.shape, 1)
    total = jnp.where(lane == width - 1, jnp.sum(loss) * (0.5 * factor), total)
    put_state(parts_ref, grad, total)


def grad_q_kernel(
    high_ref, low_ref, grad_high_ref, grad_low_ref, grad_total_ref, query_ref, state_ref, out_ref
):
    state, total = get_state(state_ref)
    total = jnp.concatenate([total] * (PAIR // total.shape[1]), axis=1)
    state = split(state)
    heads, half, _ = out_ref.shape
    tokens = query_ref.shape[0] // heads
    for k in range(query_ref.shape[0] // PAIR):
        here = slice(k * PAIR, (k + 1) * PAIR)
        grad = mxu3(state, (grad_high_ref[:, here], grad_low_ref[:, here]))
        grad = grad + total * grad_total_ref[:, here]
        feats = high_ref[:, here].astype(jnp.float32) + low_ref[:, here].astype(jnp.float32)
        inner = split(features_back_t(feats, grad))
        for n in range(PAIR // tokens):
            cut = slice(n * tokens, (n + 1) * tokens)
            query = query_ref[k * PAIR + n * tokens : k * PAIR + (n + 1) * tokens, :]
            out = mxu(inner[1][:, cut], query) + mxu(inner[0][:, cut], query)
            out_ref[k * (PAIR // tokens) + n] = out[:half] - out[half:]


def grad_k_kernel(state_ref, feats_ref, key_ref, value_ref, query_ref, out_ref):
    state, total = get_state(state_ref)
    grad = sum(mxu(term, value_ref[...], NT) for term in reversed(split(state))) + total
    inner = split(features_back_t(feats_ref[...], grad))
    out = mxu(inner[1], key_ref[...]) + mxu(inner[0], key_ref[...])
    half = out.shape[0] // 2
    heads = query_ref.shape[0]
    for h in range(heads):
        out_ref[:, h // 2, h % 2, :] = query_ref[h]
    out_ref[:, heads // 2, 0, :] = out[:half] - out[half:]
    out_ref[:, heads // 2, 1, :] = jnp.zeros((half, out.shape[1]), jnp.float32)


def total_kernel(parts_ref, loss_ref, out_ref):
    total = jnp.sum(parts_ref[...], axis=0)
    out_ref[...] = jnp.broadcast_to(total[None], out_ref.shape)
    count, last, _, width = out_ref.shape
    out_ref[:, last - 1, 1, :] = jnp.broadcast_to(loss_ref[:1], (count, width))


def finish_kernel(parts_ref, query_ref, key_ref, loss_ref):
    heads = query_ref.shape[0]
    for h in range(heads):
        query_ref[h] = parts_ref[:, h // 2, h % 2, :]
    key_ref[...] = parts_ref[:, heads // 2, 0, :]
    group = lax.axis_index("tp")
    count = lax.axis_size("tp")
    losses = parts_ref[:count, heads // 2, 1, :]
    owner = lax.rem(lax.broadcasted_iota(jnp.int32, losses.shape, 0) + group, count)
    loss_ref[...] = sum(
        jnp.sum(jnp.where(owner == k, losses, 0.0), axis=0, keepdims=True) for k in range(count)
    )


def call(kernel, out_shape, cost, grid=None, in_specs=None, out_specs=None, scratch=()):
    extra = {} if grid is None else dict(grid=grid, in_specs=in_specs, out_specs=out_specs)
    flops, nbytes = cost
    return pl.pallas_call(
        kernel,
        out_shape=out_shape,
        scratch_shapes=scratch,
        compiler_params=pltpu.CompilerParams(vmem_limit_bytes=LIMIT),
        cost_estimate=pl.CostEstimate(flops=flops, bytes_accessed=nbytes, transcendentals=0),
        **extra,
    )


def shape(*dims, dtype=jnp.float32):
    return jax.ShapeDtypeStruct(dims, dtype)


def far(*dims, dtype=jnp.float32):
    return pltpu.HBM(dims, dtype)


def keep_far(*arrays):
    return [pltpu.with_memory_space_constraint(array, pltpu.HBM) for array in arrays]


def whole(*dims):
    return pl.BlockSpec(dims, lambda i: (0,) * len(dims))


def on_device(queries, key_heads, values, target, map_q, map_k):
    tokens, heads, width = queries.shape
    count = lax.axis_size("section")
    tp_count = lax.axis_size("tp")
    count_all = float(tokens * heads * width * count * tp_count)
    key_rows = key_heads[:, 0, :]
    value_rows = values[:, 0, :]
    map_q = map_q.transpose(0, 2, 1)
    map_k = map_k.transpose(0, 2, 1)
    half = map_q.shape[1]
    feats = 2 * half
    per = heads // STEPS
    positions = heads * tokens
    low = jnp.bfloat16
    mega = 1 << 20
    by_row = pl.BlockSpec((positions // STEPS, width), lambda i: (i, 0))
    by_head = pl.BlockSpec((per, half, width), lambda i: (i, 0, 0))

    def by_lane(rows):
        return pl.BlockSpec((rows, positions // STEPS), lambda i: (0, i))

    parts_shape = shape(count, 3, width)
    with jax.named_scope("own_state"):
        packed, key_feats = call(
            key_kernel, (parts_shape, shape(feats, tokens)), (30 * mega, mega // 2)
        )(*keep_far(key_rows, value_rows, map_k))
    with jax.named_scope("states_out"):
        gathered = exchange(packed)
    halo_keys, halo_values, key_feats = lax.optimization_barrier((key_rows, value_rows, key_feats))
    halo = lax.ppermute(
        jnp.concatenate([halo_keys, halo_values], axis=0),
        "section",
        [(i, i + 1) for i in range(count - 1)],
    )
    with jax.named_scope("query_feats"):
        query_rows = queries.transpose(1, 0, 2).reshape(positions, width)
        target_rows = target.transpose(1, 0, 2).reshape(positions, width)
        pair_shape = far(feats, positions, dtype=low)
        pair = call(
            query_kernel,
            (pair_shape, pair_shape),
            (600 * mega, 3 * mega),
            (STEPS,),
            [by_row, by_head],
            [by_lane(feats)] * 2,
        )(query_rows, map_q)
    with jax.named_scope("prefix"):
        prefix = call(lambda *refs: running_kernel(False, *refs), parts_shape, (mega, mega // 4))(
            gathered
        )
        prefix, halo, query_rows, target_rows, pair = lax.optimization_barrier(
            (prefix, halo, query_rows, target_rows, pair)
        )
    with jax.named_scope("states_back"):
        returned = exchange(prefix)
    with jax.named_scope("window"):
        window = call(
            window_kernel,
            (far(width, positions), far(1, positions), far(width, positions, dtype=low)),
            (2000 * mega, 8 * mega),
            (STEPS,),
            [by_row, whole(tokens, width), whole(tokens, width), whole(2 * tokens, width), by_row],
            [by_lane(width), by_lane(1), by_lane(width)],
        )(query_rows, key_rows, value_rows, halo, target_rows)
    with jax.named_scope("student"):
        grad_shape = far(width, positions, dtype=low)
        packed, *grads = call(
            lambda *refs: student_kernel(2.0 / count_all, *refs),
            (parts_shape, grad_shape, grad_shape, far(1, positions)),
            (400 * mega, 4 * mega),
        )(*keep_far(*pair, *window), returned)
    with jax.named_scope("grads_out"):
        gathered = exchange(packed)
    with jax.named_scope("grad_q"):
        grad_q = call(
            grad_q_kernel,
            shape(heads, half, width),
            (1000 * mega, 4 * mega),
            (STEPS,),
            [by_lane(feats), by_lane(feats), by_lane(width), by_lane(width), by_lane(1)]
            + [by_row, whole(count, 3, width)],
            by_head,
        )(*keep_far(*pair, *grads, query_rows), returned)
    with jax.named_scope("suffix"):
        suffix, loss = call(
            lambda *refs: running_kernel(True, *refs),
            (parts_shape, shape(SUBLANES, width)),
            (mega, mega // 4),
        )(gathered)
    with jax.named_scope("grads_back"):
        later = exchange(suffix)
    maps_shape = shape(count, heads // 2 + 1, 2, width)

    def exchange_maps(parts):
        return exchange(parts.reshape(-1, 2, width)).reshape(parts.shape)

    with jax.named_scope("grad_k"):
        parts = call(grad_k_kernel, maps_shape, (20 * mega, mega))(
            later, key_feats, key_rows, value_rows, grad_q
        )
        parts, loss = lax.optimization_barrier((parts, loss))
    with jax.named_scope("loss_turn"):
        loss = lax.ppermute(
            loss,
            ("section", "tp"),
            [
                (s * tp_count + (t + s) % tp_count, s * tp_count + t)
                for s in range(count)
                for t in range(tp_count)
            ],
        )
    with jax.named_scope("maps_out"):
        sums = call(total_kernel, maps_shape, (mega, mega))(exchange_maps(parts), loss)
    with jax.named_scope("maps_back"):
        grad_q, grad_k, loss = call(
            finish_kernel,
            (shape(heads, half, width), shape(half, width), shape(1, width)),
            (mega, mega),
        )(exchange_maps(sums))
        grad_q = grad_q.transpose(0, 2, 1)
        grad_k = grad_k.T
        loss = loss[0, 0]
    return grad_q, grad_k[None], loss


def solution(mesh):
    in_specs = (
        P("section", "tp", None),
        P("section", "tp", None),
        P("section", "tp", None),
        P("section", "tp", None),
        P("tp", None, None),
        P("tp", None, None),
    )
    out_specs = (P("tp", None, None), P("tp", None, None), P())
    return jax.shard_map(
        on_device, mesh=mesh, in_specs=in_specs, out_specs=out_specs, check_vma=False
    )
```

```python
import math

import jax
import jax.numpy as jnp
from jax import lax
from jax.experimental import pallas as pl
from jax.experimental.pallas import tpu as pltpu
from jax.sharding import PartitionSpec as P

NN = (((1,), (0,)), ((), ()))
NT = (((1,), (1,)), ((), ()))
LIMIT = 40 * 1024 * 1024
STEPS = 2
PAIR = 256
SUBLANES = 8


def exchange(parts, axis="section"):
    return lax.all_to_all(parts, axis, 0, 0, tiled=True)


def mxu(a, b, dims=NN):
    return lax.dot_general(a, b, dims, preferred_element_type=jnp.float32)


def split(x, terms=2):
    out = []
    for _ in range(terms - 1):
        high = x.astype(jnp.bfloat16)
        out.append(high)
        x = x - high.astype(jnp.float32)
    out.append(x.astype(jnp.bfloat16))
    return out


def mxu3(a, b, dims=NN):
    return mxu(a[0], b[0], dims) + (mxu(a[0], b[1], dims) + mxu(a[1], b[0], dims))


def features_t(weight, rows):
    both = jnp.concatenate([weight, -weight], axis=0)
    proj = sum(mxu(term, rows, NT) for term in reversed(split(both, 3)))
    half = proj.shape[0] // 2
    top = jnp.max(jnp.abs(proj[:half]), axis=0, keepdims=True)
    raised = jnp.exp(proj - top)
    return raised * (1.0 / jnp.sum(raised, axis=0, keepdims=True))


def features_back_t(feats, grad):
    return feats * (grad - jnp.sum(feats * grad, axis=0, keepdims=True))


def put_state(ref, state, total):
    half = state.shape[0] // 2
    lane = lax.broadcasted_iota(jnp.int32, (half, state.shape[1]), 1)
    ref[:, 0, :] = state[:half]
    ref[:, 1, :] = state[half:]
    ref[:, 2, :] = jnp.where(lane < half, total[:half], total[half:])


def get_state(ref):
    state = jnp.concatenate([ref[:, 0, :], ref[:, 1, :]], axis=0)
    totals = ref[:, 2, :]
    half, width = totals.shape
    total = jnp.concatenate(
        [
            jnp.broadcast_to(totals[:, :1], (half, width)),
            jnp.broadcast_to(totals[:, half : half + 1], (half, width)),
        ],
        axis=0,
    )
    return state, total


def key_kernel(key_ref, value_ref, map_ref, parts_ref, feats_ref):
    feats = features_t(map_ref[0], key_ref[...])
    feats_ref[...] = feats
    state = sum(mxu(term, value_ref[...]) for term in reversed(split(feats)))
    total = jnp.broadcast_to(jnp.sum(feats, axis=1, keepdims=True), state.shape)
    put_state(parts_ref, state, total)


def running_kernel(backward, parts_ref, out_ref, *loss_ref):
    count = parts_ref.shape[0]
    row = lax.broadcasted_iota(jnp.int32, (count, count), 0)
    col = lax.broadcasted_iota(jnp.int32, (count, count), 1)
    wanted = (row + 2 <= col) if backward else (col + 2 <= row)
    chosen = jnp.where(wanted, 1.0, 0.0).astype(jnp.bfloat16)
    for k in range(parts_ref.shape[1]):
        terms = split(parts_ref[:, k, :], 3)
        out_ref[:, k, :] = sum(mxu(chosen, term) for term in reversed(terms))
    if loss_ref:
        width = parts_ref.shape[2]
        loss = jnp.sum(parts_ref[:, 2, width - 1 :], axis=0, keepdims=True)
        loss_ref[0][...] = jnp.broadcast_to(loss, loss_ref[0].shape)


def query_kernel(query_ref, map_ref, high_ref, low_ref):
    tokens = query_ref.shape[0] // map_ref.shape[0]
    for h in range(map_ref.shape[0]):
        here = slice(h * tokens, (h + 1) * tokens)
        high_ref[:, here], low_ref[:, here] = split(features_t(map_ref[h], query_ref[here, :]))


def window_kernel(
    query_ref, key_ref, value_ref, halo_ref, target_ref, sum_ref, scale_ref, target_t_ref
):
    tokens, width = key_ref.shape
    has_prev = lax.axis_index("section") > 0
    row = lax.broadcasted_iota(jnp.int32, (tokens, PAIR), 0)
    col = lax.broadcasted_iota(jnp.int32, (tokens, PAIR), 1)
    earlier = row <= lax.rem(col, tokens)
    root = 1.0 / math.sqrt(width)
    halo_keys = halo_ref[:tokens]
    halo_values_t = halo_ref[tokens:].astype(jnp.float32).T.astype(jnp.bfloat16)
    values_t = value_ref[...].astype(jnp.float32).T.astype(jnp.bfloat16)
    for k in range(query_ref.shape[0] // PAIR):
        here = slice(k * PAIR, (k + 1) * PAIR)
        query = query_ref[here, :]
        before = jnp.where(has_prev, mxu(halo_keys, query, NT) * root, -1e30)
        own = jnp.where(earlier, mxu(key_ref[...], query, NT) * root, -1e30)
        top = jnp.max(jnp.maximum(before, own), axis=0, keepdims=True)
        before = jnp.exp(before - top)
        own = jnp.exp(own - top)
        inverse = 1.0 / jnp.sum(before + own, axis=0, keepdims=True)
        total = mxu(halo_values_t, before.astype(jnp.bfloat16)) + mxu(
            values_t, own.astype(jnp.bfloat16)
        )
        sum_ref[:, here] = total * inverse
        scale_ref[:, here] = jnp.exp(-top) * inverse
        target_t_ref[:, here] = target_ref[here, :].astype(jnp.float32).T.astype(jnp.bfloat16)


def student_kernel(
    factor,
    high_ref,
    low_ref,
    sum_ref,
    scale_ref,
    target_ref,
    state_ref,
    parts_ref,
    grad_high_ref,
    grad_low_ref,
    grad_total_ref,
):
    state, total = get_state(state_ref)
    width = state.shape[1]
    extra = 2 * SUBLANES
    state = split(jnp.concatenate([state.T, total.T[:extra]], axis=0))
    grad_both = 0.0
    loss = 0.0
    for k in range(sum_ref.shape[1] // PAIR):
        here = slice(k * PAIR, (k + 1) * PAIR)
        pair = (high_ref[:, here], low_ref[:, here])
        scale = scale_ref[:, here]
        linear = mxu3(state, pair)
        inverse = 1.0 / (1.0 + scale * linear[width : width + 1])
        student = (sum_ref[:, here] + scale * linear[:width]) * inverse
        error = student - target_ref[:, here].astype(jnp.float32)
        loss = loss + jnp.sum((error * error).reshape(-1, SUBLANES, PAIR), axis=0)
        grad_sum = error * (scale * inverse * factor)
        grad_total = -jnp.sum(grad_sum * student, axis=0, keepdims=True)
        grads = split(grad_sum)
        grad_high_ref[:, here], grad_low_ref[:, here] = grads
        grad_total_ref[:, here] = grad_total
        totals = split(jnp.broadcast_to(grad_total, (extra, PAIR)))
        grads = [jnp.concatenate(both, axis=0) for both in zip(grads, totals)]
        grad_both = grad_both + mxu3(pair, grads, NT)
    grad = grad_both[:, :width]
    total = jnp.broadcast_to(grad_both[:, width : width + 1], grad.shape)
    lane = lax.broadcasted_iota(jnp.int32, total.shape, 1)
    total = jnp.where(lane == width - 1, jnp.sum(loss) * (0.5 * factor), total)
    put_state(parts_ref, grad, total)


def grad_q_kernel(
    high_ref, low_ref, grad_high_ref, grad_low_ref, grad_total_ref, query_ref, state_ref, out_ref
):
    state, total = get_state(state_ref)
    total = jnp.concatenate([total] * (PAIR // total.shape[1]), axis=1)
    state = split(state)
    _, kept, half, _ = out_ref.shape
    tokens = query_ref.shape[0] // kept
    slot = (pl.program_id(0) + lax.axis_index("section")) % 2
    for k in range(query_ref.shape[0] // PAIR):
        here = slice(k * PAIR, (k + 1) * PAIR)
        grad = mxu3(state, (grad_high_ref[:, here], grad_low_ref[:, here]))
        grad = grad + total * grad_total_ref[:, here]
        feats = high_ref[:, here].astype(jnp.float32) + low_ref[:, here].astype(jnp.float32)
        inner = split(features_back_t(feats, grad))
        for n in range(PAIR // tokens):
            cut = slice(n * tokens, (n + 1) * tokens)
            query = query_ref[k * PAIR + n * tokens : k * PAIR + (n + 1) * tokens, :]
            out = mxu(inner[1][:, cut], query) + mxu(inner[0][:, cut], query)
            out_ref[slot, k * (PAIR // tokens) + n] = out[:half] - out[half:]


def grad_k_kernel(state_ref, feats_ref, key_ref, value_ref, query_ref, other_ref, out_ref):
    state, total = get_state(state_ref)
    grad = sum(mxu(term, value_ref[...], NT) for term in reversed(split(state))) + total
    inner = split(features_back_t(feats_ref[...], grad))
    out = mxu(inner[1], key_ref[...]) + mxu(inner[0], key_ref[...])
    half = out.shape[0] // 2
    kept = query_ref.shape[1]
    for h in range(kept):
        out_ref[:, h // 2, h % 2, :] = query_ref[0, h] + other_ref[h]
    out_ref[:, kept // 2, 0, :] = out[:half] - out[half:]
    out_ref[:, kept // 2, 1, :] = jnp.zeros((half, out.shape[1]), jnp.float32)


def total_kernel(parts_ref, out_ref):
    count, last, _, width = parts_ref.shape
    parts = parts_ref[...].reshape(count // 2, 2, last, 2, width)
    total = jnp.sum(parts, axis=0)
    last = last - 1
    for n in range(2):
        out_ref[:, n * last : (n + 1) * last] = jnp.broadcast_to(
            total[n, None, :last], (count, last, 2, width)
        )
    out_ref[:, 2 * last, 0, :] = jnp.broadcast_to(total[0, last, :1] + total[1, last, :1], (count, width))
    out_ref[:, 2 * last, 1, :] = jnp.zeros((count, width), jnp.float32)


def finish_kernel(parts_ref, query_ref, key_ref):
    heads = query_ref.shape[0]
    for h in range(heads):
        query_ref[h] = parts_ref[:, h // 2, h % 2, :]
    key_ref[...] = parts_ref[:, heads // 2, 0, :]


def call(kernel, out_shape, cost, grid=None, in_specs=None, out_specs=None, scratch=()):
    extra = {} if grid is None else dict(grid=grid, in_specs=in_specs, out_specs=out_specs)
    flops, nbytes = cost
    return pl.pallas_call(
        kernel,
        out_shape=out_shape,
        scratch_shapes=scratch,
        compiler_params=pltpu.CompilerParams(vmem_limit_bytes=LIMIT),
        cost_estimate=pl.CostEstimate(flops=flops, bytes_accessed=nbytes, transcendentals=0),
        **extra,
    )


def shape(*dims, dtype=jnp.float32):
    return jax.ShapeDtypeStruct(dims, dtype)


def far(*dims, dtype=jnp.float32):
    return pltpu.HBM(dims, dtype)


def keep_far(*arrays):
    return [pltpu.with_memory_space_constraint(array, pltpu.HBM) for array in arrays]


def whole(*dims):
    return pl.BlockSpec(dims, lambda i: (0,) * len(dims))


def on_device(queries, key_heads, values, target, map_q, map_k):
    tokens, heads, width = queries.shape
    count = lax.axis_size("section")
    tp_count = lax.axis_size("tp")
    count_all = float(tokens * heads * width * count * tp_count)
    key_rows = key_heads[:, 0, :]
    value_rows = values[:, 0, :]
    map_q = map_q.transpose(0, 2, 1)
    map_k = map_k.transpose(0, 2, 1)
    half = map_q.shape[1]
    feats = 2 * half
    per = heads // STEPS
    positions = heads * tokens
    low = jnp.bfloat16
    mega = 1 << 20
    by_row = pl.BlockSpec((positions // STEPS, width), lambda i: (i, 0))
    by_head = pl.BlockSpec((per, half, width), lambda i: (i, 0, 0))

    def by_lane(rows):
        return pl.BlockSpec((rows, positions // STEPS), lambda i: (0, i))

    parts_shape = shape(count, 3, width)
    with jax.named_scope("own_state"):
        packed, key_feats = call(
            key_kernel, (parts_shape, shape(feats, tokens)), (30 * mega, mega // 2)
        )(*keep_far(key_rows, value_rows, map_k))
    with jax.named_scope("states_out"):
        gathered = exchange(packed)
    halo_keys, halo_values, key_feats = lax.optimization_barrier((key_rows, value_rows, key_feats))
    halo = lax.ppermute(
        jnp.concatenate([halo_keys, halo_values], axis=0),
        "section",
        [(i, i + 1) for i in range(count - 1)],
    )
    with jax.named_scope("query_feats"):
        query_rows = queries.transpose(1, 0, 2).reshape(positions, width)
        pair_shape = far(feats, positions, dtype=low)
        pair = call(
            query_kernel,
            (pair_shape, pair_shape),
            (600 * mega, 3 * mega),
            (STEPS,),
            [by_row, by_head],
            [by_lane(feats)] * 2,
        )(query_rows, map_q)
    with jax.named_scope("prefix"):
        prefix = call(lambda *refs: running_kernel(False, *refs), parts_shape, (mega, mega // 4))(
            gathered
        )
        prefix, halo, query_rows, target, pair = lax.optimization_barrier(
            (prefix, halo, query_rows, target, pair)
        )
    with jax.named_scope("states_back"):
        returned = exchange(prefix)
    with jax.named_scope("window"):
        target_rows = target.transpose(1, 0, 2).reshape(positions, width)
        window = call(
            window_kernel,
            (far(width, positions), far(1, positions), far(width, positions, dtype=low)),
            (2000 * mega, 8 * mega),
            (STEPS,),
            [by_row, whole(tokens, width), whole(tokens, width), whole(2 * tokens, width), by_row],
            [by_lane(width), by_lane(1), by_lane(width)],
        )(query_rows, key_rows, value_rows, halo, target_rows)
    with jax.named_scope("student"):
        grad_shape = far(width, positions, dtype=low)
        packed, *grads = call(
            lambda *refs: student_kernel(2.0 / count_all, *refs),
            (parts_shape, grad_shape, grad_shape, far(1, positions)),
            (400 * mega, 4 * mega),
        )(*keep_far(*pair, *window), returned)
    with jax.named_scope("grads_out"):
        gathered = exchange(packed)
    with jax.named_scope("grad_q"):
        grad_q = call(
            grad_q_kernel,
            shape(2, heads // 2, half, width),
            (1000 * mega, 4 * mega),
            (STEPS,),
            [by_lane(feats), by_lane(feats), by_lane(width), by_lane(width), by_lane(1)]
            + [by_row, whole(count, 3, width)],
            whole(2, heads // 2, half, width),
        )(*keep_far(*pair, *grads, query_rows), returned)
    with jax.named_scope("grad_q_swap"):
        other = lax.ppermute(grad_q[1], "section", [(i, i ^ 1) for i in range(count)])
    with jax.named_scope("suffix"):
        gathered, grad_q = lax.optimization_barrier((gathered, grad_q))
        suffix, loss = call(
            lambda *refs: running_kernel(True, *refs),
            (parts_shape, shape(SUBLANES, width)),
            (mega, mega // 4),
        )(gathered)
    with jax.named_scope("grads_back"):
        later = exchange(suffix)
    def over_tp(loss, bit):
        return loss + lax.ppermute(loss, "tp", [(i, i ^ bit) for i in range(tp_count)])

    with jax.named_scope("loss_core"):
        loss = over_tp(loss, 1)
        later, loss = lax.optimization_barrier((later, loss))
    sent_shape = shape(count, heads // 4 + 1, 2, width)
    maps_shape = shape(count, heads // 2 + 1, 2, width)

    def exchange_maps(parts):
        return exchange(parts.reshape(-1, 2, width)).reshape(parts.shape)

    with jax.named_scope("grad_k"):
        parts = call(grad_k_kernel, sent_shape, (20 * mega, mega))(
            later, key_feats, key_rows, value_rows, grad_q, other
        )
        parts, loss = lax.optimization_barrier((parts, loss))
    with jax.named_scope("loss_near"):
        loss = over_tp(loss, 2)
    with jax.named_scope("maps_out"):
        parts, loss = lax.optimization_barrier((exchange_maps(parts), loss))
        sums = call(total_kernel, maps_shape, (mega, mega))(parts)
        sums, loss = lax.optimization_barrier((sums, loss))
    with jax.named_scope("loss_far"):
        loss = over_tp(loss, 4)
    with jax.named_scope("maps_back"):
        grad_q, grad_k = call(
            finish_kernel, (shape(heads, half, width), shape(half, width)), (mega, mega)
        )(exchange_maps(sums))
        grad_q = grad_q.transpose(0, 2, 1)
        grad_k = grad_k.T
        loss = loss[0, 0]
    return grad_q, grad_k[None], loss


def solution(mesh):
    in_specs = (
        P("section", "tp", None),
        P("section", "tp", None),
        P("section", "tp", None),
        P("section", "tp", None),
        P("tp", None, None),
        P("tp", None, None),
    )
    out_specs = (P("tp", None, None), P("tp", None, None), P())
    return jax.shard_map(
        on_device, mesh=mesh, in_specs=in_specs, out_specs=out_specs, check_vma=False
    )
```

```python
import math

import jax
import jax.numpy as jnp
from jax import lax
from jax.experimental import pallas as pl
from jax.experimental.pallas import tpu as pltpu
from jax.sharding import PartitionSpec as P

NN = (((1,), (0,)), ((), ()))
NT = (((1,), (1,)), ((), ()))
LIMIT = 40 * 1024 * 1024
STEPS = 2
PAIR = 256
SUBLANES = 8


def exchange(parts, axis="section"):
    return lax.all_to_all(parts, axis, 0, 0, tiled=True)


def mxu(a, b, dims=NN):
    return lax.dot_general(a, b, dims, preferred_element_type=jnp.float32)


def split(x, terms=2):
    out = []
    for _ in range(terms - 1):
        high = x.astype(jnp.bfloat16)
        out.append(high)
        x = x - high.astype(jnp.float32)
    out.append(x.astype(jnp.bfloat16))
    return out


def mxu3(a, b, dims=NN):
    return mxu(a[0], b[0], dims) + (mxu(a[0], b[1], dims) + mxu(a[1], b[0], dims))


def features_t(weight, rows):
    both = jnp.concatenate([weight, -weight], axis=0)
    proj = sum(mxu(term, rows, NT) for term in reversed(split(both, 3)))
    half = proj.shape[0] // 2
    top = jnp.max(jnp.abs(proj[:half]), axis=0, keepdims=True)
    raised = jnp.exp(proj - top)
    return raised * (1.0 / jnp.sum(raised, axis=0, keepdims=True))


def features_back_t(feats, grad):
    return feats * (grad - jnp.sum(feats * grad, axis=0, keepdims=True))


def put_state(ref, state, total):
    half = state.shape[0] // 2
    lane = lax.broadcasted_iota(jnp.int32, (half, state.shape[1]), 1)
    ref[:, 0, :] = state[:half]
    ref[:, 1, :] = state[half:]
    ref[:, 2, :] = jnp.where(lane < half, total[:half], total[half:])


def get_state(ref):
    state = jnp.concatenate([ref[:, 0, :], ref[:, 1, :]], axis=0)
    totals = ref[:, 2, :]
    half, width = totals.shape
    total = jnp.concatenate(
        [
            jnp.broadcast_to(totals[:, :1], (half, width)),
            jnp.broadcast_to(totals[:, half : half + 1], (half, width)),
        ],
        axis=0,
    )
    return state, total


def key_kernel(key_ref, value_ref, map_ref, parts_ref, feats_ref):
    feats = features_t(map_ref[0], key_ref[...])
    feats_ref[...] = feats
    state = sum(mxu(term, value_ref[...]) for term in reversed(split(feats)))
    total = jnp.broadcast_to(jnp.sum(feats, axis=1, keepdims=True), state.shape)
    put_state(parts_ref, state, total)


def running_kernel(backward, parts_ref, out_ref, *loss_ref):
    count = parts_ref.shape[0]
    row = lax.broadcasted_iota(jnp.int32, (count, count), 0)
    col = lax.broadcasted_iota(jnp.int32, (count, count), 1)
    wanted = (row + 2 <= col) if backward else (col + 2 <= row)
    chosen = jnp.where(wanted, 1.0, 0.0).astype(jnp.bfloat16)
    for k in range(parts_ref.shape[1]):
        terms = split(parts_ref[:, k, :], 3)
        out_ref[:, k, :] = sum(mxu(chosen, term) for term in reversed(terms))
    if loss_ref:
        width = parts_ref.shape[2]
        loss = jnp.sum(parts_ref[:, 2, width - 1 :], axis=0, keepdims=True)
        loss_ref[0][...] = jnp.broadcast_to(loss, loss_ref[0].shape)


def query_kernel(query_ref, map_ref, high_ref, low_ref):
    tokens = query_ref.shape[0] // map_ref.shape[0]
    for h in range(map_ref.shape[0]):
        here = slice(h * tokens, (h + 1) * tokens)
        high_ref[:, here], low_ref[:, here] = split(features_t(map_ref[h], query_ref[here, :]))


def window_kernel(
    query_ref, key_ref, value_ref, halo_ref, target_ref, sum_ref, scale_ref, target_t_ref
):
    tokens, width = key_ref.shape
    has_prev = lax.axis_index("section") > 0
    row = lax.broadcasted_iota(jnp.int32, (tokens, PAIR), 0)
    col = lax.broadcasted_iota(jnp.int32, (tokens, PAIR), 1)
    earlier = row <= lax.rem(col, tokens)
    root = 1.0 / math.sqrt(width)
    halo_keys = halo_ref[:tokens]
    halo_values_t = halo_ref[tokens:].astype(jnp.float32).T.astype(jnp.bfloat16)
    values_t = value_ref[...].astype(jnp.float32).T.astype(jnp.bfloat16)
    for k in range(query_ref.shape[0] // PAIR):
        here = slice(k * PAIR, (k + 1) * PAIR)
        query = query_ref[here, :]
        before = jnp.where(has_prev, mxu(halo_keys, query, NT) * root, -1e30)
        own = jnp.where(earlier, mxu(key_ref[...], query, NT) * root, -1e30)
        top = jnp.max(jnp.maximum(before, own), axis=0, keepdims=True)
        before = jnp.exp(before - top)
        own = jnp.exp(own - top)
        inverse = 1.0 / jnp.sum(before + own, axis=0, keepdims=True)
        total = mxu(halo_values_t, before.astype(jnp.bfloat16)) + mxu(
            values_t, own.astype(jnp.bfloat16)
        )
        sum_ref[:, here] = total * inverse
        scale_ref[:, here] = jnp.exp(-top) * inverse
        target_t_ref[:, here] = target_ref[here, :].astype(jnp.float32).T.astype(jnp.bfloat16)


def student_kernel(
    factor,
    high_ref,
    low_ref,
    sum_ref,
    scale_ref,
    target_ref,
    state_ref,
    parts_ref,
    grad_high_ref,
    grad_low_ref,
    grad_total_ref,
):
    state, total = get_state(state_ref)
    width = state.shape[1]
    extra = 2 * SUBLANES
    state = split(jnp.concatenate([state.T, total.T[:extra]], axis=0))
    grad_both = 0.0
    loss = 0.0
    for k in range(sum_ref.shape[1] // PAIR):
        here = slice(k * PAIR, (k + 1) * PAIR)
        pair = (high_ref[:, here], low_ref[:, here])
        scale = scale_ref[:, here]
        linear = mxu3(state, pair)
        inverse = 1.0 / (1.0 + scale * linear[width : width + 1])
        student = (sum_ref[:, here] + scale * linear[:width]) * inverse
        error = student - target_ref[:, here].astype(jnp.float32)
        loss = loss + jnp.sum((error * error).reshape(-1, SUBLANES, PAIR), axis=0)
        grad_sum = error * (scale * inverse * factor)
        grad_total = -jnp.sum(grad_sum * student, axis=0, keepdims=True)
        grads = split(grad_sum)
        grad_high_ref[:, here], grad_low_ref[:, here] = grads
        grad_total_ref[:, here] = grad_total
        totals = split(jnp.broadcast_to(grad_total, (extra, PAIR)))
        grads = [jnp.concatenate(both, axis=0) for both in zip(grads, totals)]
        grad_both = grad_both + mxu3(pair, grads, NT)
    grad = grad_both[:, :width]
    total = jnp.broadcast_to(grad_both[:, width : width + 1], grad.shape)
    lane = lax.broadcasted_iota(jnp.int32, total.shape, 1)
    total = jnp.where(lane == width - 1, jnp.sum(loss) * (0.5 * factor), total)
    put_state(parts_ref, grad, total)


def grad_q_kernel(
    high_ref, low_ref, grad_high_ref, grad_low_ref, grad_total_ref, query_ref, state_ref, out_ref
):
    state, total = get_state(state_ref)
    total = jnp.concatenate([total] * (PAIR // total.shape[1]), axis=1)
    state = split(state)
    _, kept, half, _ = out_ref.shape
    tokens = query_ref.shape[0] // kept
    slot = (pl.program_id(0) + lax.axis_index("section")) % 2
    for k in range(query_ref.shape[0] // PAIR):
        here = slice(k * PAIR, (k + 1) * PAIR)
        grad = mxu3(state, (grad_high_ref[:, here], grad_low_ref[:, here]))
        grad = grad + total * grad_total_ref[:, here]
        feats = high_ref[:, here].astype(jnp.float32) + low_ref[:, here].astype(jnp.float32)
        inner = split(features_back_t(feats, grad))
        for n in range(PAIR // tokens):
            cut = slice(n * tokens, (n + 1) * tokens)
            query = query_ref[k * PAIR + n * tokens : k * PAIR + (n + 1) * tokens, :]
            out = mxu(inner[1][:, cut], query) + mxu(inner[0][:, cut], query)
            out_ref[slot, k * (PAIR // tokens) + n] = out[:half] - out[half:]


def grad_k_kernel(state_ref, feats_ref, key_ref, value_ref, query_ref, other_ref, out_ref):
    state, total = get_state(state_ref)
    grad = sum(mxu(term, value_ref[...], NT) for term in reversed(split(state))) + total
    inner = split(features_back_t(feats_ref[...], grad))
    out = mxu(inner[1], key_ref[...]) + mxu(inner[0], key_ref[...])
    half = out.shape[0] // 2
    kept = query_ref.shape[1]
    for h in range(kept):
        out_ref[:, h // 2, h % 2, :] = query_ref[0, h] + other_ref[h]
    out_ref[:, kept // 2, 0, :] = out[:half] - out[half:]
    out_ref[:, kept // 2, 1, :] = jnp.zeros((half, out.shape[1]), jnp.float32)


def total_kernel(parts_ref, out_ref):
    count, last, _, width = parts_ref.shape
    parts = parts_ref[...].reshape(count // 2, 2, last, 2, width)
    total = jnp.sum(parts, axis=0)
    last = last - 1
    for n in range(2):
        out_ref[:, n * last : (n + 1) * last] = jnp.broadcast_to(
            total[n, None, :last], (count, last, 2, width)
        )
    out_ref[:, 2 * last, 0, :] = jnp.broadcast_to(total[0, last, :1] + total[1, last, :1], (count, width))
    out_ref[:, 2 * last, 1, :] = jnp.zeros((count, width), jnp.float32)


def finish_kernel(parts_ref, query_ref, key_ref):
    heads = query_ref.shape[0]
    for h in range(heads):
        query_ref[h] = parts_ref[:, h // 2, h % 2, :]
    key_ref[...] = parts_ref[:, heads // 2, 0, :]


def call(kernel, out_shape, cost, grid=None, in_specs=None, out_specs=None, scratch=()):
    extra = {} if grid is None else dict(grid=grid, in_specs=in_specs, out_specs=out_specs)
    flops, nbytes = cost
    return pl.pallas_call(
        kernel,
        out_shape=out_shape,
        scratch_shapes=scratch,
        compiler_params=pltpu.CompilerParams(vmem_limit_bytes=LIMIT),
        cost_estimate=pl.CostEstimate(flops=flops, bytes_accessed=nbytes, transcendentals=0),
        **extra,
    )


def shape(*dims, dtype=jnp.float32):
    return jax.ShapeDtypeStruct(dims, dtype)


def far(*dims, dtype=jnp.float32):
    return pltpu.HBM(dims, dtype)


def keep_far(*arrays):
    return [pltpu.with_memory_space_constraint(array, pltpu.HBM) for array in arrays]


def whole(*dims):
    return pl.BlockSpec(dims, lambda i: (0,) * len(dims))


def on_device(queries, key_heads, values, target, map_q, map_k):
    tokens, heads, width = queries.shape
    count = lax.axis_size("section")
    tp_count = lax.axis_size("tp")
    count_all = float(tokens * heads * width * count * tp_count)
    key_rows = key_heads[:, 0, :]
    value_rows = values[:, 0, :]
    map_q = map_q.transpose(0, 2, 1)
    map_k = map_k.transpose(0, 2, 1)
    half = map_q.shape[1]
    feats = 2 * half
    per = heads // STEPS
    positions = heads * tokens
    low = jnp.bfloat16
    mega = 1 << 20
    by_row = pl.BlockSpec((positions // STEPS, width), lambda i: (i, 0))
    by_head = pl.BlockSpec((per, half, width), lambda i: (i, 0, 0))

    def by_lane(rows):
        return pl.BlockSpec((rows, positions // STEPS), lambda i: (0, i))

    parts_shape = shape(count, 3, width)
    with jax.named_scope("own_state"):
        packed, key_feats = call(
            key_kernel, (parts_shape, shape(feats, tokens)), (30 * mega, mega // 2)
        )(*keep_far(key_rows, value_rows, map_k))
    with jax.named_scope("states_out"):
        gathered = exchange(packed)
    halo_keys, halo_values, key_feats = lax.optimization_barrier((key_rows, value_rows, key_feats))
    halo = lax.ppermute(
        jnp.concatenate([halo_keys, halo_values], axis=0),
        "section",
        [(i, i + 1) for i in range(count - 1)],
    )
    with jax.named_scope("query_feats"):
        query_rows = queries.transpose(1, 0, 2).reshape(positions, width)
        pair_shape = far(feats, positions, dtype=low)
        pair = call(
            query_kernel,
            (pair_shape, pair_shape),
            (600 * mega, 3 * mega),
            (STEPS,),
            [by_row, by_head],
            [by_lane(feats)] * 2,
        )(query_rows, map_q)
    with jax.named_scope("prefix"):
        prefix = call(lambda *refs: running_kernel(False, *refs), parts_shape, (mega, mega // 4))(
            gathered
        )
        prefix, halo, query_rows, target, pair = lax.optimization_barrier(
            (prefix, halo, query_rows, target, pair)
        )
    with jax.named_scope("states_back"):
        returned = exchange(prefix)
    with jax.named_scope("window"):
        target_rows = target.transpose(1, 0, 2).reshape(positions, width)
        window = call(
            window_kernel,
            (far(width, positions), far(1, positions), far(width, positions, dtype=low)),
            (2000 * mega, 8 * mega),
            (STEPS,),
            [by_row, whole(tokens, width), whole(tokens, width), whole(2 * tokens, width), by_row],
            [by_lane(width), by_lane(1), by_lane(width)],
        )(query_rows, key_rows, value_rows, halo, target_rows)
    with jax.named_scope("student"):
        grad_shape = far(width, positions, dtype=low)
        packed, *grads = call(
            lambda *refs: student_kernel(2.0 / count_all, *refs),
            (parts_shape, grad_shape, grad_shape, far(1, positions)),
            (400 * mega, 4 * mega),
        )(*keep_far(*pair, *window), returned)
    with jax.named_scope("grads_out"):
        gathered = exchange(packed)
    with jax.named_scope("grad_q"):
        grad_q = call(
            grad_q_kernel,
            shape(2, heads // 2, half, width),
            (1000 * mega, 4 * mega),
            (STEPS,),
            [by_lane(feats), by_lane(feats), by_lane(width), by_lane(width), by_lane(1)]
            + [by_row, whole(count, 3, width)],
            whole(2, heads // 2, half, width),
        )(*keep_far(*pair, *grads, query_rows), returned)
    with jax.named_scope("grad_q_swap"):
        other = lax.ppermute(grad_q[1], "section", [(i, i ^ 1) for i in range(count)])
    with jax.named_scope("suffix"):
        gathered, grad_q = lax.optimization_barrier((gathered, grad_q))
        suffix, loss = call(
            lambda *refs: running_kernel(True, *refs),
            (parts_shape, shape(SUBLANES, width)),
            (mega, mega // 4),
        )(gathered)
    with jax.named_scope("grads_back"):
        later = exchange(suffix)
    def over_tp(loss, bit):
        return loss + lax.ppermute(loss, "tp", [(i, i ^ bit) for i in range(tp_count)])

    sent_shape = shape(count, heads // 4 + 1, 2, width)
    maps_shape = shape(count, heads // 2 + 1, 2, width)

    def exchange_maps(parts):
        return exchange(parts.reshape(-1, 2, width)).reshape(parts.shape)

    with jax.named_scope("grad_k"):
        parts = call(grad_k_kernel, sent_shape, (20 * mega, mega))(
            later, key_feats, key_rows, value_rows, grad_q, other
        )
        parts, loss = lax.optimization_barrier((parts, loss))
    with jax.named_scope("loss_near"):
        loss = over_tp(loss, 2)
    with jax.named_scope("maps_out"):
        parts, loss = lax.optimization_barrier((exchange_maps(parts), loss))
        sums = call(total_kernel, maps_shape, (mega, mega))(parts)
        sums, loss = lax.optimization_barrier((sums, loss))
    with jax.named_scope("loss_far"):
        loss = over_tp(over_tp(loss, 1), 4)
    with jax.named_scope("maps_back"):
        grad_q, grad_k = call(
            finish_kernel, (shape(heads, half, width), shape(half, width)), (mega, mega)
        )(exchange_maps(sums))
        grad_q = grad_q.transpose(0, 2, 1)
        grad_k = grad_k.T
        loss = loss[0, 0]
    return grad_q, grad_k[None], loss


def solution(mesh):
    in_specs = (
        P("section", "tp", None),
        P("section", "tp", None),
        P("section", "tp", None),
        P("section", "tp", None),
        P("tp", None, None),
        P("tp", None, None),
    )
    out_specs = (P("tp", None, None), P("tp", None, None), P())
    return jax.shard_map(
        on_device, mesh=mesh, in_specs=in_specs, out_specs=out_specs, check_vma=False
    )
```

```python
import math

import jax
import jax.numpy as jnp
from jax import lax
from jax.experimental import pallas as pl
from jax.experimental.pallas import tpu as pltpu
from jax.sharding import PartitionSpec as P

NN = (((1,), (0,)), ((), ()))
NT = (((1,), (1,)), ((), ()))
LIMIT = 40 * 1024 * 1024
STEPS = 2
PAIR = 256
SUBLANES = 8


def exchange(parts, axis="section"):
    return lax.all_to_all(parts, axis, 0, 0, tiled=True)


def mxu(a, b, dims=NN):
    return lax.dot_general(a, b, dims, preferred_element_type=jnp.float32)


def split(x, terms=2):
    out = []
    for _ in range(terms - 1):
        high = x.astype(jnp.bfloat16)
        out.append(high)
        x = x - high.astype(jnp.float32)
    out.append(x.astype(jnp.bfloat16))
    return out


def mxu3(a, b, dims=NN):
    return mxu(a[0], b[0], dims) + (mxu(a[0], b[1], dims) + mxu(a[1], b[0], dims))


def features_t(weight, rows):
    both = jnp.concatenate([weight, -weight], axis=0)
    proj = sum(mxu(term, rows, NT) for term in reversed(split(both, 3)))
    half = proj.shape[0] // 2
    top = jnp.max(jnp.abs(proj[:half]), axis=0, keepdims=True)
    raised = jnp.exp(proj - top)
    return raised * (1.0 / jnp.sum(raised, axis=0, keepdims=True))


def features_back_t(feats, grad):
    return feats * (grad - jnp.sum(feats * grad, axis=0, keepdims=True))


def put_state(ref, state, total):
    half = state.shape[0] // 2
    lane = lax.broadcasted_iota(jnp.int32, (half, state.shape[1]), 1)
    ref[:, 0, :] = state[:half]
    ref[:, 1, :] = state[half:]
    ref[:, 2, :] = jnp.where(lane < half, total[:half], total[half:])


def get_state(ref):
    state = jnp.concatenate([ref[:, 0, :], ref[:, 1, :]], axis=0)
    totals = ref[:, 2, :]
    half, width = totals.shape
    total = jnp.concatenate(
        [
            jnp.broadcast_to(totals[:, :1], (half, width)),
            jnp.broadcast_to(totals[:, half : half + 1], (half, width)),
        ],
        axis=0,
    )
    return state, total


def key_kernel(key_ref, value_ref, map_ref, parts_ref, feats_ref):
    feats = features_t(map_ref[0], key_ref[...])
    feats_ref[...] = feats
    state = sum(mxu(term, value_ref[...]) for term in reversed(split(feats)))
    total = jnp.broadcast_to(jnp.sum(feats, axis=1, keepdims=True), state.shape)
    put_state(parts_ref, state, total)


def running_kernel(backward, parts_ref, out_ref, *loss_ref):
    count = parts_ref.shape[0]
    row = lax.broadcasted_iota(jnp.int32, (count, count), 0)
    col = lax.broadcasted_iota(jnp.int32, (count, count), 1)
    wanted = (row + 2 <= col) if backward else (col + 2 <= row)
    chosen = jnp.where(wanted, 1.0, 0.0).astype(jnp.bfloat16)
    for k in range(parts_ref.shape[1]):
        terms = split(parts_ref[:, k, :], 3)
        out_ref[:, k, :] = sum(mxu(chosen, term) for term in reversed(terms))
    if loss_ref:
        width = parts_ref.shape[2]
        loss = jnp.sum(parts_ref[:, 2, width - 1 :], axis=0, keepdims=True)
        loss_ref[0][...] = jnp.broadcast_to(loss, loss_ref[0].shape)


def query_kernel(query_ref, map_ref, high_ref, low_ref):
    tokens = query_ref.shape[0] // map_ref.shape[0]
    for h in range(map_ref.shape[0]):
        here = slice(h * tokens, (h + 1) * tokens)
        high_ref[:, here], low_ref[:, here] = split(features_t(map_ref[h], query_ref[here, :]))


def window_kernel(
    query_ref, key_ref, value_ref, halo_ref, target_ref, sum_ref, scale_ref, target_t_ref
):
    tokens, width = key_ref.shape
    has_prev = lax.axis_index("section") > 0
    row = lax.broadcasted_iota(jnp.int32, (tokens, PAIR), 0)
    col = lax.broadcasted_iota(jnp.int32, (tokens, PAIR), 1)
    earlier = row <= lax.rem(col, tokens)
    root = 1.0 / math.sqrt(width)
    halo_keys = halo_ref[:tokens]
    halo_values_t = halo_ref[tokens:].astype(jnp.float32).T.astype(jnp.bfloat16)
    values_t = value_ref[...].astype(jnp.float32).T.astype(jnp.bfloat16)
    for k in range(query_ref.shape[0] // PAIR):
        here = slice(k * PAIR, (k + 1) * PAIR)
        query = query_ref[here, :]
        before = jnp.where(has_prev, mxu(halo_keys, query, NT) * root, -1e30)
        own = jnp.where(earlier, mxu(key_ref[...], query, NT) * root, -1e30)
        top = jnp.max(jnp.maximum(before, own), axis=0, keepdims=True)
        before = jnp.exp(before - top)
        own = jnp.exp(own - top)
        inverse = 1.0 / jnp.sum(before + own, axis=0, keepdims=True)
        total = mxu(halo_values_t, before.astype(jnp.bfloat16)) + mxu(
            values_t, own.astype(jnp.bfloat16)
        )
        sum_ref[:, here] = total * inverse
        scale_ref[:, here] = jnp.exp(-top) * inverse
        target_t_ref[:, here] = target_ref[here, :].astype(jnp.float32).T.astype(jnp.bfloat16)


def student_kernel(
    factor,
    high_ref,
    low_ref,
    sum_ref,
    scale_ref,
    target_ref,
    state_ref,
    parts_ref,
    grad_high_ref,
    grad_low_ref,
    grad_total_ref,
):
    state, total = get_state(state_ref)
    width = state.shape[1]
    extra = 2 * SUBLANES
    state = split(jnp.concatenate([state.T, total.T[:extra]], axis=0))
    grad_both = 0.0
    loss = 0.0
    for k in range(sum_ref.shape[1] // PAIR):
        here = slice(k * PAIR, (k + 1) * PAIR)
        pair = (high_ref[:, here], low_ref[:, here])
        scale = scale_ref[:, here]
        linear = mxu3(state, pair)
        inverse = 1.0 / (1.0 + scale * linear[width : width + 1])
        student = (sum_ref[:, here] + scale * linear[:width]) * inverse
        error = student - target_ref[:, here].astype(jnp.float32)
        loss = loss + jnp.sum((error * error).reshape(-1, SUBLANES, PAIR), axis=0)
        grad_sum = error * (scale * inverse * factor)
        grad_total = -jnp.sum(grad_sum * student, axis=0, keepdims=True)
        grads = split(grad_sum)
        grad_high_ref[:, here], grad_low_ref[:, here] = grads
        grad_total_ref[:, here] = grad_total
        totals = split(jnp.broadcast_to(grad_total, (extra, PAIR)))
        grads = [jnp.concatenate(both, axis=0) for both in zip(grads, totals)]
        grad_both = grad_both + mxu3(pair, grads, NT)
    grad = grad_both[:, :width]
    total = jnp.broadcast_to(grad_both[:, width : width + 1], grad.shape)
    lane = lax.broadcasted_iota(jnp.int32, total.shape, 1)
    total = jnp.where(lane == width - 1, jnp.sum(loss) * (0.5 * factor), total)
    put_state(parts_ref, grad, total)


def grad_q_kernel(
    high_ref, low_ref, grad_high_ref, grad_low_ref, grad_total_ref, query_ref, state_ref, out_ref
):
    state, total = get_state(state_ref)
    total = jnp.concatenate([total] * (PAIR // total.shape[1]), axis=1)
    state = split(state)
    _, kept, half, _ = out_ref.shape
    tokens = query_ref.shape[0] // kept
    slot = (pl.program_id(0) + lax.axis_index("section")) % 2
    for k in range(query_ref.shape[0] // PAIR):
        here = slice(k * PAIR, (k + 1) * PAIR)
        grad = mxu3(state, (grad_high_ref[:, here], grad_low_ref[:, here]))
        grad = grad + total * grad_total_ref[:, here]
        feats = high_ref[:, here].astype(jnp.float32) + low_ref[:, here].astype(jnp.float32)
        inner = split(features_back_t(feats, grad))
        for n in range(PAIR // tokens):
            cut = slice(n * tokens, (n + 1) * tokens)
            query = query_ref[k * PAIR + n * tokens : k * PAIR + (n + 1) * tokens, :]
            out = mxu(inner[1][:, cut], query) + mxu(inner[0][:, cut], query)
            out_ref[slot, k * (PAIR // tokens) + n] = out[:half] - out[half:]


def grad_k_kernel(state_ref, feats_ref, key_ref, value_ref, query_ref, other_ref, out_ref):
    state, total = get_state(state_ref)
    grad = sum(mxu(term, value_ref[...], NT) for term in reversed(split(state))) + total
    inner = split(features_back_t(feats_ref[...], grad))
    out = mxu(inner[1], key_ref[...]) + mxu(inner[0], key_ref[...])
    half = out.shape[0] // 2
    kept = query_ref.shape[1]
    for h in range(kept):
        out_ref[:, h // 2, h % 2, :] = query_ref[0, h] + other_ref[h]
    out_ref[:, kept // 2, 0, :] = out[:half] - out[half:]
    out_ref[:, kept // 2, 1, :] = jnp.zeros((half, out.shape[1]), jnp.float32)


def total_kernel(parts_ref, out_ref):
    count, last, _, width = parts_ref.shape
    parts = parts_ref[...].reshape(count // 2, 2, last, 2, width)
    total = jnp.sum(parts, axis=0)
    last = last - 1
    for n in range(2):
        out_ref[:, n * last : (n + 1) * last] = jnp.broadcast_to(
            total[n, None, :last], (count, last, 2, width)
        )
    out_ref[:, 2 * last, 0, :] = jnp.broadcast_to(total[0, last, :1] + total[1, last, :1], (count, width))
    out_ref[:, 2 * last, 1, :] = jnp.zeros((count, width), jnp.float32)


def finish_kernel(parts_ref, query_ref, key_ref):
    heads = query_ref.shape[0]
    for h in range(heads):
        query_ref[h] = parts_ref[:, h // 2, h % 2, :]
    key_ref[...] = parts_ref[:, heads // 2, 0, :]


def call(kernel, out_shape, cost, grid=None, in_specs=None, out_specs=None, scratch=()):
    extra = {} if grid is None else dict(grid=grid, in_specs=in_specs, out_specs=out_specs)
    flops, nbytes = cost
    return pl.pallas_call(
        kernel,
        out_shape=out_shape,
        scratch_shapes=scratch,
        compiler_params=pltpu.CompilerParams(vmem_limit_bytes=LIMIT),
        cost_estimate=pl.CostEstimate(flops=flops, bytes_accessed=nbytes, transcendentals=0),
        **extra,
    )


def shape(*dims, dtype=jnp.float32):
    return jax.ShapeDtypeStruct(dims, dtype)


def far(*dims, dtype=jnp.float32):
    return pltpu.HBM(dims, dtype)


def keep_far(*arrays):
    return [pltpu.with_memory_space_constraint(array, pltpu.HBM) for array in arrays]


def whole(*dims):
    return pl.BlockSpec(dims, lambda i: (0,) * len(dims))


def on_device(queries, key_heads, values, target, map_q, map_k):
    tokens, heads, width = queries.shape
    count = lax.axis_size("section")
    tp_count = lax.axis_size("tp")
    count_all = float(tokens * heads * width * count * tp_count)
    key_rows = key_heads[:, 0, :]
    value_rows = values[:, 0, :]
    map_q = map_q.transpose(0, 2, 1)
    map_k = map_k.transpose(0, 2, 1)
    half = map_q.shape[1]
    feats = 2 * half
    per = heads // STEPS
    positions = heads * tokens
    low = jnp.bfloat16
    mega = 1 << 20
    by_row = pl.BlockSpec((positions // STEPS, width), lambda i: (i, 0))
    by_head = pl.BlockSpec((per, half, width), lambda i: (i, 0, 0))

    def by_lane(rows):
        return pl.BlockSpec((rows, positions // STEPS), lambda i: (0, i))

    parts_shape = shape(count, 3, width)
    with jax.named_scope("own_state"):
        packed, key_feats = call(
            key_kernel, (parts_shape, shape(feats, tokens)), (30 * mega, mega // 2)
        )(*keep_far(key_rows, value_rows, map_k))
    with jax.named_scope("states_out"):
        gathered = exchange(packed)
    halo_keys, halo_values, key_feats = lax.optimization_barrier((key_rows, value_rows, key_feats))
    halo = lax.ppermute(
        jnp.concatenate([halo_keys, halo_values], axis=0),
        "section",
        [(i, i + 1) for i in range(count - 1)],
    )
    with jax.named_scope("query_feats"):
        query_rows = queries.transpose(1, 0, 2).reshape(positions, width)
        pair_shape = far(feats, positions, dtype=low)
        pair = call(
            query_kernel,
            (pair_shape, pair_shape),
            (600 * mega, 3 * mega),
            (STEPS,),
            [by_row, by_head],
            [by_lane(feats)] * 2,
        )(query_rows, map_q)
    with jax.named_scope("prefix"):
        prefix = call(lambda *refs: running_kernel(False, *refs), parts_shape, (mega, mega // 4))(
            gathered
        )
        prefix, halo, query_rows, target, pair = lax.optimization_barrier(
            (prefix, halo, query_rows, target, pair)
        )
    with jax.named_scope("states_back"):
        returned = exchange(prefix)
    with jax.named_scope("window"):
        target_rows = target.transpose(1, 0, 2).reshape(positions, width)
        window = call(
            window_kernel,
            (far(width, positions), far(1, positions), far(width, positions, dtype=low)),
            (2000 * mega, 8 * mega),
            (STEPS,),
            [by_row, whole(tokens, width), whole(tokens, width), whole(2 * tokens, width), by_row],
            [by_lane(width), by_lane(1), by_lane(width)],
        )(query_rows, key_rows, value_rows, halo, target_rows)
    with jax.named_scope("student"):
        grad_shape = far(width, positions, dtype=low)
        packed, *grads = call(
            lambda *refs: student_kernel(2.0 / count_all, *refs),
            (parts_shape, grad_shape, grad_shape, far(1, positions)),
            (400 * mega, 4 * mega),
        )(*pair, *keep_far(*window), returned)
    with jax.named_scope("grads_out"):
        gathered = exchange(packed)
    with jax.named_scope("grad_q"):
        grad_q = call(
            grad_q_kernel,
            shape(2, heads // 2, half, width),
            (1000 * mega, 4 * mega),
            (STEPS,),
            [by_lane(feats), by_lane(feats), by_lane(width), by_lane(width), by_lane(1)]
            + [by_row, whole(count, 3, width)],
            whole(2, heads // 2, half, width),
        )(*keep_far(*pair, *grads, query_rows), returned)
    with jax.named_scope("grad_q_swap"):
        other = lax.ppermute(grad_q[1], "section", [(i, i ^ 1) for i in range(count)])
    with jax.named_scope("suffix"):
        gathered, grad_q = lax.optimization_barrier((gathered, grad_q))
        suffix, loss = call(
            lambda *refs: running_kernel(True, *refs),
            (parts_shape, shape(SUBLANES, width)),
            (mega, mega // 4),
        )(gathered)
    with jax.named_scope("grads_back"):
        later = exchange(suffix)
    def over_tp(loss, bit):
        return loss + lax.ppermute(loss, "tp", [(i, i ^ bit) for i in range(tp_count)])

    sent_shape = shape(count, heads // 4 + 1, 2, width)
    maps_shape = shape(count, heads // 2 + 1, 2, width)

    def exchange_maps(parts):
        return exchange(parts.reshape(-1, 2, width)).reshape(parts.shape)

    with jax.named_scope("grad_k"):
        parts = call(grad_k_kernel, sent_shape, (20 * mega, mega))(
            later, key_feats, key_rows, value_rows, grad_q, other
        )
        parts, loss = lax.optimization_barrier((parts, loss))
    with jax.named_scope("loss_near"):
        loss = over_tp(loss, 2)
    with jax.named_scope("maps_out"):
        parts, loss = lax.optimization_barrier((exchange_maps(parts), loss))
        sums = call(total_kernel, maps_shape, (mega, mega))(parts)
        sums, loss = lax.optimization_barrier((sums, loss))
    with jax.named_scope("loss_far"):
        loss = over_tp(over_tp(loss, 1), tp_count - 2)
    with jax.named_scope("maps_back"):
        grad_q, grad_k = call(
            finish_kernel, (shape(heads, half, width), shape(half, width)), (mega, mega)
        )(exchange_maps(sums))
        grad_q = grad_q.transpose(0, 2, 1)
        grad_k = grad_k.T
        loss = loss[0, 0]
    return grad_q, grad_k[None], loss


def solution(mesh):
    in_specs = (
        P("section", "tp", None),
        P("section", "tp", None),
        P("section", "tp", None),
        P("section", "tp", None),
        P("tp", None, None),
        P("tp", None, None),
    )
    out_specs = (P("tp", None, None), P("tp", None, None), P())
    return jax.shard_map(
        on_device, mesh=mesh, in_specs=in_specs, out_specs=out_specs, check_vma=False
    )
```

```python
import math

import jax
import jax.numpy as jnp
from jax import lax
from jax.experimental import pallas as pl
from jax.experimental.pallas import tpu as pltpu
from jax.sharding import PartitionSpec as P

NN = (((1,), (0,)), ((), ()))
NT = (((1,), (1,)), ((), ()))
LIMIT = 40 * 1024 * 1024
STEPS = 2
PAIR = 256
SUBLANES = 8


def exchange(parts, axis="section"):
    return lax.all_to_all(parts, axis, 0, 0, tiled=True)


def mxu(a, b, dims=NN):
    return lax.dot_general(a, b, dims, preferred_element_type=jnp.float32)


def split(x, terms=2):
    out = []
    for _ in range(terms - 1):
        high = x.astype(jnp.bfloat16)
        out.append(high)
        x = x - high.astype(jnp.float32)
    out.append(x.astype(jnp.bfloat16))
    return out


def mxu3(a, b, dims=NN):
    return mxu(a[0], b[0], dims) + (mxu(a[0], b[1], dims) + mxu(a[1], b[0], dims))


def features_t(weight, rows):
    both = jnp.concatenate([weight, -weight], axis=0)
    proj = sum(mxu(term, rows, NT) for term in reversed(split(both, 3)))
    half = proj.shape[0] // 2
    top = jnp.max(jnp.abs(proj[:half]), axis=0, keepdims=True)
    raised = jnp.exp(proj - top)
    return raised * (1.0 / jnp.sum(raised, axis=0, keepdims=True))


def features_back_t(feats, grad):
    return feats * (grad - jnp.sum(feats * grad, axis=0, keepdims=True))


def put_state(ref, state, total):
    half = state.shape[0] // 2
    lane = lax.broadcasted_iota(jnp.int32, (half, state.shape[1]), 1)
    ref[:, 0, :] = state[:half]
    ref[:, 1, :] = state[half:]
    ref[:, 2, :] = jnp.where(lane < half, total[:half], total[half:])


def get_state(ref):
    state = jnp.concatenate([ref[:, 0, :], ref[:, 1, :]], axis=0)
    totals = ref[:, 2, :]
    half, width = totals.shape
    total = jnp.concatenate(
        [
            jnp.broadcast_to(totals[:, :1], (half, width)),
            jnp.broadcast_to(totals[:, half : half + 1], (half, width)),
        ],
        axis=0,
    )
    return state, total


def key_kernel(key_ref, value_ref, map_ref, parts_ref, feats_ref):
    feats = features_t(map_ref[0], key_ref[...])
    feats_ref[...] = feats
    state = sum(mxu(term, value_ref[...]) for term in reversed(split(feats)))
    total = jnp.broadcast_to(jnp.sum(feats, axis=1, keepdims=True), state.shape)
    put_state(parts_ref, state, total)


def running_kernel(backward, parts_ref, out_ref, *loss_ref):
    count = parts_ref.shape[0]
    row = lax.broadcasted_iota(jnp.int32, (count, count), 0)
    col = lax.broadcasted_iota(jnp.int32, (count, count), 1)
    wanted = (row + 2 <= col) if backward else (col + 2 <= row)
    chosen = jnp.where(wanted, 1.0, 0.0).astype(jnp.bfloat16)
    for k in range(parts_ref.shape[1]):
        terms = split(parts_ref[:, k, :], 3)
        out_ref[:, k, :] = sum(mxu(chosen, term) for term in reversed(terms))
    if loss_ref:
        width = parts_ref.shape[2]
        loss = jnp.sum(parts_ref[:, 2, width - 1 :], axis=0, keepdims=True)
        loss_ref[0][...] = jnp.broadcast_to(loss, loss_ref[0].shape)


def query_kernel(query_ref, map_ref, high_ref, low_ref):
    tokens = query_ref.shape[0] // map_ref.shape[0]
    for h in range(map_ref.shape[0]):
        here = slice(h * tokens, (h + 1) * tokens)
        high_ref[:, here], low_ref[:, here] = split(features_t(map_ref[h], query_ref[here, :]))


def window_kernel(
    query_ref, key_ref, value_ref, halo_ref, target_ref, sum_ref, scale_ref, target_t_ref
):
    tokens, width = key_ref.shape
    has_prev = lax.axis_index("section") > 0
    row = lax.broadcasted_iota(jnp.int32, (tokens, PAIR), 0)
    col = lax.broadcasted_iota(jnp.int32, (tokens, PAIR), 1)
    earlier = row <= lax.rem(col, tokens)
    root = 1.0 / math.sqrt(width)
    halo_keys = halo_ref[:tokens]
    halo_values_t = halo_ref[tokens:].astype(jnp.float32).T.astype(jnp.bfloat16)
    values_t = value_ref[...].astype(jnp.float32).T.astype(jnp.bfloat16)
    for k in range(query_ref.shape[0] // PAIR):
        here = slice(k * PAIR, (k + 1) * PAIR)
        query = query_ref[here, :]
        before = jnp.where(has_prev, mxu(halo_keys, query, NT) * root, -1e30)
        own = jnp.where(earlier, mxu(key_ref[...], query, NT) * root, -1e30)
        top = jnp.max(jnp.maximum(before, own), axis=0, keepdims=True)
        before = jnp.exp(before - top)
        own = jnp.exp(own - top)
        inverse = 1.0 / jnp.sum(before + own, axis=0, keepdims=True)
        total = mxu(halo_values_t, before.astype(jnp.bfloat16)) + mxu(
            values_t, own.astype(jnp.bfloat16)
        )
        sum_ref[:, here] = total * inverse
        scale_ref[:, here] = jnp.exp(-top) * inverse
        target_t_ref[:, here] = target_ref[here, :].astype(jnp.float32).T.astype(jnp.bfloat16)


def student_kernel(
    factor,
    high_ref,
    low_ref,
    sum_ref,
    scale_ref,
    target_ref,
    state_ref,
    parts_ref,
    grad_high_ref,
    grad_low_ref,
    grad_total_ref,
):
    state, total = get_state(state_ref)
    width = state.shape[1]
    extra = 2 * SUBLANES
    state = split(jnp.concatenate([state.T, total.T[:extra]], axis=0))
    grad_both = 0.0
    loss = 0.0
    for k in range(sum_ref.shape[1] // PAIR):
        here = slice(k * PAIR, (k + 1) * PAIR)
        pair = (high_ref[:, here], low_ref[:, here])
        scale = scale_ref[:, here]
        linear = mxu3(state, pair)
        inverse = 1.0 / (1.0 + scale * linear[width : width + 1])
        student = (sum_ref[:, here] + scale * linear[:width]) * inverse
        error = student - target_ref[:, here].astype(jnp.float32)
        loss = loss + jnp.sum((error * error).reshape(-1, SUBLANES, PAIR), axis=0)
        grad_sum = error * (scale * inverse * factor)
        grad_total = -jnp.sum(grad_sum * student, axis=0, keepdims=True)
        grads = split(grad_sum)
        grad_high_ref[:, here], grad_low_ref[:, here] = grads
        grad_total_ref[:, here] = grad_total
        totals = split(jnp.broadcast_to(grad_total, (extra, PAIR)))
        grads = [jnp.concatenate(both, axis=0) for both in zip(grads, totals)]
        grad_both = grad_both + mxu3(pair, grads, NT)
    grad = grad_both[:, :width]
    total = jnp.broadcast_to(grad_both[:, width : width + 1], grad.shape)
    lane = lax.broadcasted_iota(jnp.int32, total.shape, 1)
    total = jnp.where(lane == width - 1, jnp.sum(loss) * (0.5 * factor), total)
    put_state(parts_ref, grad, total)


def grad_q_kernel(
    _, high_ref, low_ref, grad_high_ref, grad_low_ref, grad_total_ref, query_ref, state_ref, out_ref
):
    state, total = get_state(state_ref)
    total = jnp.concatenate([total] * (PAIR // total.shape[1]), axis=1)
    state = split(state)
    kept, half, _ = out_ref.shape
    tokens = query_ref.shape[0] // kept
    for k in range(query_ref.shape[0] // PAIR):
        here = slice(k * PAIR, (k + 1) * PAIR)
        grad = mxu3(state, (grad_high_ref[:, here], grad_low_ref[:, here]))
        grad = grad + total * grad_total_ref[:, here]
        feats = high_ref[:, here].astype(jnp.float32) + low_ref[:, here].astype(jnp.float32)
        inner = split(features_back_t(feats, grad))
        for n in range(PAIR // tokens):
            cut = slice(n * tokens, (n + 1) * tokens)
            query = query_ref[k * PAIR + n * tokens : k * PAIR + (n + 1) * tokens, :]
            out = mxu(inner[1][:, cut], query) + mxu(inner[0][:, cut], query)
            out_ref[k * (PAIR // tokens) + n] = out[:half] - out[half:]


def grad_k_kernel(state_ref, feats_ref, key_ref, value_ref, query_ref, other_ref, out_ref):
    state, total = get_state(state_ref)
    grad = sum(mxu(term, value_ref[...], NT) for term in reversed(split(state))) + total
    inner = split(features_back_t(feats_ref[...], grad))
    out = mxu(inner[1], key_ref[...]) + mxu(inner[0], key_ref[...])
    half = out.shape[0] // 2
    kept = query_ref.shape[0]
    for h in range(kept):
        out_ref[:, h // 2, h % 2, :] = query_ref[h] + other_ref[h]
    out_ref[:, kept // 2, 0, :] = out[:half] - out[half:]
    out_ref[:, kept // 2, 1, :] = jnp.zeros((half, out.shape[1]), jnp.float32)


def total_kernel(parts_ref, out_ref):
    count, last, _, width = parts_ref.shape
    parts = parts_ref[...].reshape(count // 2, 2, last, 2, width)
    total = jnp.sum(parts, axis=0)
    last = last - 1
    for n in range(2):
        out_ref[:, n * last : (n + 1) * last] = jnp.broadcast_to(
            total[n, None, :last], (count, last, 2, width)
        )
    out_ref[:, 2 * last, 0, :] = jnp.broadcast_to(total[0, last, :1] + total[1, last, :1], (count, width))
    out_ref[:, 2 * last, 1, :] = jnp.zeros((count, width), jnp.float32)


def finish_kernel(parts_ref, query_ref, key_ref):
    heads = query_ref.shape[0]
    for h in range(heads):
        query_ref[h] = parts_ref[:, h // 2, h % 2, :]
    key_ref[...] = parts_ref[:, heads // 2, 0, :]


def call(kernel, out_shape, cost, grid=None, in_specs=None, out_specs=None, scratch=()):
    extra = {} if grid is None else dict(grid=grid, in_specs=in_specs, out_specs=out_specs)
    flops, nbytes = cost
    return pl.pallas_call(
        kernel,
        out_shape=out_shape,
        scratch_shapes=scratch,
        compiler_params=pltpu.CompilerParams(vmem_limit_bytes=LIMIT),
        cost_estimate=pl.CostEstimate(flops=flops, bytes_accessed=nbytes, transcendentals=0),
        **extra,
    )


def shape(*dims, dtype=jnp.float32):
    return jax.ShapeDtypeStruct(dims, dtype)


def far(*dims, dtype=jnp.float32):
    return pltpu.HBM(dims, dtype)


def keep_far(*arrays):
    return [pltpu.with_memory_space_constraint(array, pltpu.HBM) for array in arrays]


def whole(*dims):
    return pl.BlockSpec(dims, lambda i: (0,) * len(dims))


def on_device(queries, key_heads, values, target, map_q, map_k):
    tokens, heads, width = queries.shape
    count = lax.axis_size("section")
    tp_count = lax.axis_size("tp")
    count_all = float(tokens * heads * width * count * tp_count)
    key_rows = key_heads[:, 0, :]
    value_rows = values[:, 0, :]
    map_q = map_q.transpose(0, 2, 1)
    map_k = map_k.transpose(0, 2, 1)
    half = map_q.shape[1]
    feats = 2 * half
    per = heads // STEPS
    positions = heads * tokens
    low = jnp.bfloat16
    mega = 1 << 20
    by_row = pl.BlockSpec((positions // STEPS, width), lambda i: (i, 0))
    by_head = pl.BlockSpec((per, half, width), lambda i: (i, 0, 0))

    def by_lane(rows):
        return pl.BlockSpec((rows, positions // STEPS), lambda i: (0, i))

    parts_shape = shape(count, 3, width)
    with jax.named_scope("own_state"):
        packed, key_feats = call(
            key_kernel, (parts_shape, shape(feats, tokens)), (30 * mega, mega // 2)
        )(*keep_far(key_rows, value_rows, map_k))
    with jax.named_scope("states_out"):
        gathered = exchange(packed)
    halo_keys, halo_values, key_feats = lax.optimization_barrier((key_rows, value_rows, key_feats))
    halo = lax.ppermute(
        jnp.concatenate([halo_keys, halo_values], axis=0),
        "section",
        [(i, i + 1) for i in range(count - 1)],
    )
    with jax.named_scope("query_feats"):
        query_rows = queries.transpose(1, 0, 2).reshape(positions, width)
        pair_shape = far(feats, positions, dtype=low)
        pair = call(
            query_kernel,
            (pair_shape, pair_shape),
            (600 * mega, 3 * mega),
            (STEPS,),
            [by_row, by_head],
            [by_lane(feats)] * 2,
        )(query_rows, map_q)
    with jax.named_scope("prefix"):
        prefix = call(lambda *refs: running_kernel(False, *refs), parts_shape, (mega, mega // 4))(
            gathered
        )
        prefix, halo, query_rows, target, pair = lax.optimization_barrier(
            (prefix, halo, query_rows, target, pair)
        )
    with jax.named_scope("states_back"):
        returned = exchange(prefix)
    with jax.named_scope("window"):
        target_rows = target.transpose(1, 0, 2).reshape(positions, width)
        window = call(
            window_kernel,
            (far(width, positions), far(1, positions), far(width, positions, dtype=low)),
            (2000 * mega, 8 * mega),
            (STEPS,),
            [by_row, whole(tokens, width), whole(tokens, width), whole(2 * tokens, width), by_row],
            [by_lane(width), by_lane(1), by_lane(width)],
        )(query_rows, key_rows, value_rows, halo, target_rows)
    with jax.named_scope("student"):
        grad_shape = far(width, positions, dtype=low)
        packed, *grads = call(
            lambda *refs: student_kernel(2.0 / count_all, *refs),
            (parts_shape, grad_shape, grad_shape, far(1, positions)),
            (400 * mega, 4 * mega),
        )(*pair, *keep_far(*window), returned)
    with jax.named_scope("grads_out"):
        gathered = exchange(packed)
    with jax.named_scope("grad_q"):
        cut = positions // 2

        def lane_half(rows):
            return pl.BlockSpec((rows, cut), lambda i, which: (0, which[0]))

        def grad_q_half(which):
            return pl.pallas_call(
                grad_q_kernel,
                out_shape=shape(heads // 2, half, width),
                grid_spec=pltpu.PrefetchScalarGridSpec(
                    num_scalar_prefetch=1,
                    grid=(1,),
                    in_specs=[lane_half(feats)] * 2
                    + [lane_half(width)] * 2
                    + [
                        lane_half(1),
                        pl.BlockSpec((cut, width), lambda i, which: (which[0], 0)),
                        pl.BlockSpec((count, 3, width), lambda i, which: (0, 0, 0)),
                    ],
                    out_specs=pl.BlockSpec((heads // 2, half, width), lambda i, which: (0, 0, 0)),
                ),
                compiler_params=pltpu.CompilerParams(vmem_limit_bytes=LIMIT),
                cost_estimate=pl.CostEstimate(
                    flops=500 * mega, bytes_accessed=2 * mega, transcendentals=0
                ),
            )(which[None], *keep_far(*pair, *grads, query_rows), returned)

        mine = lax.axis_index("section") % 2
        sent = grad_q_half(1 - mine)
    with jax.named_scope("grad_q_swap"):
        other = lax.ppermute(sent, "section", [(i, i ^ 1) for i in range(count)])
    with jax.named_scope("suffix"):
        gathered, sent = lax.optimization_barrier((gathered, sent))
        suffix, loss = call(
            lambda *refs: running_kernel(True, *refs),
            (parts_shape, shape(SUBLANES, width)),
            (mega, mega // 4),
        )(gathered)
        suffix, mine = lax.optimization_barrier((suffix, mine))
    with jax.named_scope("grad_q_kept"):
        grad_q = grad_q_half(mine)
    with jax.named_scope("grads_back"):
        later = exchange(suffix)
    def over_tp(loss, bit):
        return loss + lax.ppermute(loss, "tp", [(i, i ^ bit) for i in range(tp_count)])

    sent_shape = shape(count, heads // 4 + 1, 2, width)
    maps_shape = shape(count, heads // 2 + 1, 2, width)

    def exchange_maps(parts):
        return exchange(parts.reshape(-1, 2, width)).reshape(parts.shape)

    with jax.named_scope("grad_k"):
        parts = call(grad_k_kernel, sent_shape, (20 * mega, mega))(
            later, key_feats, key_rows, value_rows, grad_q, other
        )
        parts, loss = lax.optimization_barrier((parts, loss))
    with jax.named_scope("loss_near"):
        loss = over_tp(loss, 2)
    with jax.named_scope("maps_out"):
        parts, loss = lax.optimization_barrier((exchange_maps(parts), loss))
        sums = call(total_kernel, maps_shape, (mega, mega))(parts)
        sums, loss = lax.optimization_barrier((sums, loss))
    with jax.named_scope("loss_far"):
        loss = over_tp(over_tp(loss, 1), tp_count - 2)
    with jax.named_scope("maps_back"):
        grad_q, grad_k = call(
            finish_kernel, (shape(heads, half, width), shape(half, width)), (mega, mega)
        )(exchange_maps(sums))
        grad_q = grad_q.transpose(0, 2, 1)
        grad_k = grad_k.T
        loss = loss[0, 0]
    return grad_q, grad_k[None], loss


def solution(mesh):
    in_specs = (
        P("section", "tp", None),
        P("section", "tp", None),
        P("section", "tp", None),
        P("section", "tp", None),
        P("tp", None, None),
        P("tp", None, None),
    )
    out_specs = (P("tp", None, None), P("tp", None, None), P())
    return jax.shard_map(
        on_device, mesh=mesh, in_specs=in_specs, out_specs=out_specs, check_vma=False
    )
```

```python
import math

import jax
import jax.numpy as jnp
from jax import lax
from jax.experimental import pallas as pl
from jax.experimental.pallas import tpu as pltpu
from jax.sharding import PartitionSpec as P

NN = (((1,), (0,)), ((), ()))
NT = (((1,), (1,)), ((), ()))
LIMIT = 40 * 1024 * 1024
STEPS = 2
PAIR = 256
SUBLANES = 8


def exchange(parts, axis="section"):
    return lax.all_to_all(parts, axis, 0, 0, tiled=True)


def mxu(a, b, dims=NN):
    return lax.dot_general(a, b, dims, preferred_element_type=jnp.float32)


def split(x, terms=2):
    out = []
    for _ in range(terms - 1):
        high = x.astype(jnp.bfloat16)
        out.append(high)
        x = x - high.astype(jnp.float32)
    out.append(x.astype(jnp.bfloat16))
    return out


def mxu3(a, b, dims=NN):
    return mxu(a[0], b[0], dims) + (mxu(a[0], b[1], dims) + mxu(a[1], b[0], dims))


def features_t(weight, rows):
    both = jnp.concatenate([weight, -weight], axis=0)
    proj = sum(mxu(term, rows, NT) for term in reversed(split(both, 3)))
    half = proj.shape[0] // 2
    top = jnp.max(jnp.abs(proj[:half]), axis=0, keepdims=True)
    raised = jnp.exp(proj - top)
    return raised * (1.0 / jnp.sum(raised, axis=0, keepdims=True))


def features_back_t(feats, grad):
    return feats * (grad - jnp.sum(feats * grad, axis=0, keepdims=True))


def put_state(ref, state, total):
    half = state.shape[0] // 2
    lane = lax.broadcasted_iota(jnp.int32, (half, state.shape[1]), 1)
    ref[:, 0, :] = state[:half]
    ref[:, 1, :] = state[half:]
    ref[:, 2, :] = jnp.where(lane < half, total[:half], total[half:])


def get_state(ref):
    state = jnp.concatenate([ref[:, 0, :], ref[:, 1, :]], axis=0)
    totals = ref[:, 2, :]
    half, width = totals.shape
    total = jnp.concatenate(
        [
            jnp.broadcast_to(totals[:, :1], (half, width)),
            jnp.broadcast_to(totals[:, half : half + 1], (half, width)),
        ],
        axis=0,
    )
    return state, total


def key_kernel(key_ref, value_ref, map_ref, parts_ref, feats_ref):
    feats = features_t(map_ref[0], key_ref[...])
    feats_ref[...] = feats
    state = sum(mxu(term, value_ref[...]) for term in reversed(split(feats)))
    total = jnp.broadcast_to(jnp.sum(feats, axis=1, keepdims=True), state.shape)
    put_state(parts_ref, state, total)


def running_kernel(backward, parts_ref, out_ref, *loss_ref):
    count = parts_ref.shape[0]
    row = lax.broadcasted_iota(jnp.int32, (count, count), 0)
    col = lax.broadcasted_iota(jnp.int32, (count, count), 1)
    wanted = (row + 2 <= col) if backward else (col + 2 <= row)
    chosen = jnp.where(wanted, 1.0, 0.0).astype(jnp.bfloat16)
    for k in range(parts_ref.shape[1]):
        terms = split(parts_ref[:, k, :], 3)
        out_ref[:, k, :] = sum(mxu(chosen, term) for term in reversed(terms))
    if loss_ref:
        width = parts_ref.shape[2]
        loss = jnp.sum(parts_ref[:, 2, width - 1 :], axis=0, keepdims=True)
        loss_ref[0][...] = jnp.broadcast_to(loss, loss_ref[0].shape)


def query_kernel(query_ref, map_ref, high_ref, low_ref):
    tokens = query_ref.shape[0] // map_ref.shape[0]
    for h in range(map_ref.shape[0]):
        here = slice(h * tokens, (h + 1) * tokens)
        high_ref[:, here], low_ref[:, here] = split(features_t(map_ref[h], query_ref[here, :]))


def window_kernel(
    query_ref, key_ref, value_ref, halo_ref, target_ref, sum_ref, scale_ref, target_t_ref
):
    tokens, width = key_ref.shape
    has_prev = lax.axis_index("section") > 0
    row = lax.broadcasted_iota(jnp.int32, (tokens, PAIR), 0)
    col = lax.broadcasted_iota(jnp.int32, (tokens, PAIR), 1)
    earlier = row <= lax.rem(col, tokens)
    root = 1.0 / math.sqrt(width)
    halo_keys = halo_ref[:tokens]
    halo_values_t = halo_ref[tokens:].astype(jnp.float32).T.astype(jnp.bfloat16)
    values_t = value_ref[...].astype(jnp.float32).T.astype(jnp.bfloat16)
    for k in range(query_ref.shape[0] // PAIR):
        here = slice(k * PAIR, (k + 1) * PAIR)
        query = query_ref[here, :]
        before = jnp.where(has_prev, mxu(halo_keys, query, NT) * root, -1e30)
        own = jnp.where(earlier, mxu(key_ref[...], query, NT) * root, -1e30)
        top = jnp.max(jnp.maximum(before, own), axis=0, keepdims=True)
        before = jnp.exp(before - top)
        own = jnp.exp(own - top)
        inverse = 1.0 / jnp.sum(before + own, axis=0, keepdims=True)
        total = mxu(halo_values_t, before.astype(jnp.bfloat16)) + mxu(
            values_t, own.astype(jnp.bfloat16)
        )
        sum_ref[:, here] = total * inverse
        scale_ref[:, here] = jnp.exp(-top) * inverse
        target_t_ref[:, here] = target_ref[here, :].astype(jnp.float32).T.astype(jnp.bfloat16)


def student_kernel(
    factor,
    high_ref,
    low_ref,
    sum_ref,
    scale_ref,
    target_ref,
    state_ref,
    parts_ref,
    grad_high_ref,
    grad_low_ref,
    grad_total_ref,
):
    state, total = get_state(state_ref)
    width = state.shape[1]
    extra = 2 * SUBLANES
    state = split(jnp.concatenate([state.T, total.T[:extra]], axis=0))
    grad_both = 0.0
    loss = 0.0
    for k in range(sum_ref.shape[1] // PAIR):
        here = slice(k * PAIR, (k + 1) * PAIR)
        pair = (high_ref[:, here], low_ref[:, here])
        scale = scale_ref[:, here]
        linear = mxu3(state, pair)
        inverse = 1.0 / (1.0 + scale * linear[width : width + 1])
        student = (sum_ref[:, here] + scale * linear[:width]) * inverse
        error = student - target_ref[:, here].astype(jnp.float32)
        loss = loss + jnp.sum((error * error).reshape(-1, SUBLANES, PAIR), axis=0)
        grad_sum = error * (scale * inverse * factor)
        grad_total = -jnp.sum(grad_sum * student, axis=0, keepdims=True)
        grads = split(grad_sum)
        grad_high_ref[:, here], grad_low_ref[:, here] = grads
        grad_total_ref[:, here] = grad_total
        totals = split(jnp.broadcast_to(grad_total, (extra, PAIR)))
        grads = [jnp.concatenate(both, axis=0) for both in zip(grads, totals)]
        grad_both = grad_both + mxu3(pair, grads, NT)
    grad = grad_both[:, :width]
    total = jnp.broadcast_to(grad_both[:, width : width + 1], grad.shape)
    lane = lax.broadcasted_iota(jnp.int32, total.shape, 1)
    total = jnp.where(lane == width - 1, jnp.sum(loss) * (0.5 * factor), total)
    put_state(parts_ref, grad, total)


def grad_q_kernel(
    _, high_ref, low_ref, grad_high_ref, grad_low_ref, grad_total_ref, query_ref, state_ref, out_ref
):
    state, total = get_state(state_ref)
    total = jnp.concatenate([total] * (PAIR // total.shape[1]), axis=1)
    state = split(state)
    kept, half, _ = out_ref.shape
    tokens = query_ref.shape[0] // kept
    for k in range(query_ref.shape[0] // PAIR):
        here = slice(k * PAIR, (k + 1) * PAIR)
        grad = mxu3(state, (grad_high_ref[:, here], grad_low_ref[:, here]))
        grad = grad + total * grad_total_ref[:, here]
        feats = high_ref[:, here].astype(jnp.float32) + low_ref[:, here].astype(jnp.float32)
        inner = split(features_back_t(feats, grad))
        for n in range(PAIR // tokens):
            cut = slice(n * tokens, (n + 1) * tokens)
            query = query_ref[k * PAIR + n * tokens : k * PAIR + (n + 1) * tokens, :]
            out = mxu(inner[1][:, cut], query) + mxu(inner[0][:, cut], query)
            out_ref[k * (PAIR // tokens) + n] = out[:half] - out[half:]


def grad_k_kernel(state_ref, feats_ref, key_ref, value_ref, query_ref, other_ref, out_ref):
    state, total = get_state(state_ref)
    grad = sum(mxu(term, value_ref[...], NT) for term in reversed(split(state))) + total
    inner = split(features_back_t(feats_ref[...], grad))
    out = mxu(inner[1], key_ref[...]) + mxu(inner[0], key_ref[...])
    half = out.shape[0] // 2
    kept = query_ref.shape[0]
    for h in range(kept):
        out_ref[:, h // 2, h % 2, :] = query_ref[h] + other_ref[h]
    out_ref[:, kept // 2, 0, :] = out[:half] - out[half:]
    out_ref[:, kept // 2, 1, :] = jnp.zeros((half, out.shape[1]), jnp.float32)


def total_kernel(parts_ref, out_ref):
    count, last, _, width = parts_ref.shape
    parts = parts_ref[...].reshape(count // 2, 2, last, 2, width)
    total = jnp.sum(parts, axis=0)
    last = last - 1
    for n in range(2):
        out_ref[:, n * last : (n + 1) * last] = jnp.broadcast_to(
            total[n, None, :last], (count, last, 2, width)
        )
    out_ref[:, 2 * last, 0, :] = jnp.broadcast_to(total[0, last, :1] + total[1, last, :1], (count, width))
    out_ref[:, 2 * last, 1, :] = jnp.zeros((count, width), jnp.float32)


def finish_kernel(parts_ref, query_ref, key_ref):
    heads = query_ref.shape[0]
    first = pl.program_id(0) * (heads // 2)
    for h in range(heads):
        query_ref[h] = parts_ref[:, first + h // 2, h % 2, :]
    key_ref[...] = parts_ref[:, parts_ref.shape[1] - 1, 0, :]


def call(kernel, out_shape, cost, grid=None, in_specs=None, out_specs=None, scratch=()):
    extra = {} if grid is None else dict(grid=grid, in_specs=in_specs, out_specs=out_specs)
    flops, nbytes = cost
    return pl.pallas_call(
        kernel,
        out_shape=out_shape,
        scratch_shapes=scratch,
        compiler_params=pltpu.CompilerParams(vmem_limit_bytes=LIMIT),
        cost_estimate=pl.CostEstimate(flops=flops, bytes_accessed=nbytes, transcendentals=0),
        **extra,
    )


def shape(*dims, dtype=jnp.float32):
    return jax.ShapeDtypeStruct(dims, dtype)


def far(*dims, dtype=jnp.float32):
    return pltpu.HBM(dims, dtype)


def keep_far(*arrays):
    return [pltpu.with_memory_space_constraint(array, pltpu.HBM) for array in arrays]


def whole(*dims):
    return pl.BlockSpec(dims, lambda i: (0,) * len(dims))


def on_device(queries, key_heads, values, target, map_q, map_k):
    tokens, heads, width = queries.shape
    count = lax.axis_size("section")
    tp_count = lax.axis_size("tp")
    count_all = float(tokens * heads * width * count * tp_count)
    key_rows = key_heads[:, 0, :]
    value_rows = values[:, 0, :]
    map_q = map_q.transpose(0, 2, 1)
    map_k = map_k.transpose(0, 2, 1)
    half = map_q.shape[1]
    feats = 2 * half
    per = heads // STEPS
    positions = heads * tokens
    low = jnp.bfloat16
    mega = 1 << 20
    by_row = pl.BlockSpec((positions // STEPS, width), lambda i: (i, 0))
    by_head = pl.BlockSpec((per, half, width), lambda i: (i, 0, 0))

    def by_lane(rows):
        return pl.BlockSpec((rows, positions // STEPS), lambda i: (0, i))

    parts_shape = shape(count, 3, width)
    with jax.named_scope("own_state"):
        packed, key_feats = call(
            key_kernel, (parts_shape, shape(feats, tokens)), (30 * mega, mega // 2)
        )(*keep_far(key_rows, value_rows, map_k))
    with jax.named_scope("states_out"):
        gathered = exchange(packed)
    halo_keys, halo_values, key_feats = lax.optimization_barrier((key_rows, value_rows, key_feats))
    halo = lax.ppermute(
        jnp.concatenate([halo_keys, halo_values], axis=0),
        "section",
        [(i, i + 1) for i in range(count - 1)],
    )
    with jax.named_scope("query_feats"):
        query_rows = queries.transpose(1, 0, 2).reshape(positions, width)
        pair_shape = far(feats, positions, dtype=low)
        pair = call(
            query_kernel,
            (pair_shape, pair_shape),
            (600 * mega, 3 * mega),
            (STEPS,),
            [by_row, by_head],
            [by_lane(feats)] * 2,
        )(query_rows, map_q)
    with jax.named_scope("prefix"):
        prefix = call(lambda *refs: running_kernel(False, *refs), parts_shape, (mega, mega // 4))(
            gathered
        )
        prefix, halo, query_rows, target, pair = lax.optimization_barrier(
            (prefix, halo, query_rows, target, pair)
        )
    with jax.named_scope("states_back"):
        returned = exchange(prefix)
    with jax.named_scope("window"):
        target_rows = target.transpose(1, 0, 2).reshape(positions, width)
        window = call(
            window_kernel,
            (far(width, positions), far(1, positions), far(width, positions, dtype=low)),
            (2000 * mega, 8 * mega),
            (STEPS,),
            [by_row, whole(tokens, width), whole(tokens, width), whole(2 * tokens, width), by_row],
            [by_lane(width), by_lane(1), by_lane(width)],
        )(query_rows, key_rows, value_rows, halo, target_rows)
    with jax.named_scope("student"):
        grad_shape = far(width, positions, dtype=low)
        packed, *grads = call(
            lambda *refs: student_kernel(2.0 / count_all, *refs),
            (parts_shape, grad_shape, grad_shape, far(1, positions)),
            (400 * mega, 4 * mega),
        )(*pair, *keep_far(*window), returned)
    with jax.named_scope("grads_out"):
        gathered = exchange(packed)
    with jax.named_scope("grad_q"):
        cut = positions // 2

        def lane_half(rows):
            return pl.BlockSpec((rows, cut), lambda i, which: (0, which[0]))

        def grad_q_half(which):
            return pl.pallas_call(
                grad_q_kernel,
                out_shape=shape(heads // 2, half, width),
                grid_spec=pltpu.PrefetchScalarGridSpec(
                    num_scalar_prefetch=1,
                    grid=(1,),
                    in_specs=[lane_half(feats)] * 2
                    + [lane_half(width)] * 2
                    + [
                        lane_half(1),
                        pl.BlockSpec((cut, width), lambda i, which: (which[0], 0)),
                        pl.BlockSpec((count, 3, width), lambda i, which: (0, 0, 0)),
                    ],
                    out_specs=pl.BlockSpec((heads // 2, half, width), lambda i, which: (0, 0, 0)),
                ),
                compiler_params=pltpu.CompilerParams(vmem_limit_bytes=LIMIT),
                cost_estimate=pl.CostEstimate(
                    flops=500 * mega, bytes_accessed=2 * mega, transcendentals=0
                ),
            )(which[None], *keep_far(*pair, *grads, query_rows), returned)

        mine = lax.axis_index("section") % 2
        sent = grad_q_half(1 - mine)
    with jax.named_scope("grad_q_swap"):
        other = lax.ppermute(sent, "section", [(i, i ^ 1) for i in range(count)])
    with jax.named_scope("suffix"):
        gathered, sent = lax.optimization_barrier((gathered, sent))
        suffix, loss = call(
            lambda *refs: running_kernel(True, *refs),
            (parts_shape, shape(SUBLANES, width)),
            (mega, mega // 4),
        )(gathered)
        suffix, mine = lax.optimization_barrier((suffix, mine))
    with jax.named_scope("grad_q_kept"):
        grad_q = grad_q_half(mine)
    with jax.named_scope("grads_back"):
        later = exchange(suffix)
    def over_tp(loss, bit):
        return loss + lax.ppermute(loss, "tp", [(i, i ^ bit) for i in range(tp_count)])

    sent_shape = shape(count, heads // 4 + 1, 2, width)
    maps_shape = shape(count, heads // 2 + 1, 2, width)

    def exchange_maps(parts):
        return exchange(parts.reshape(-1, 2, width)).reshape(parts.shape)

    with jax.named_scope("grad_k"):
        parts = call(grad_k_kernel, sent_shape, (20 * mega, mega))(
            later, key_feats, key_rows, value_rows, grad_q, other
        )
        parts, loss = lax.optimization_barrier((parts, loss))
    with jax.named_scope("loss_near"):
        loss = over_tp(loss, 2)
    with jax.named_scope("maps_out"):
        parts, loss = lax.optimization_barrier((exchange_maps(parts), loss))
        sums = call(total_kernel, maps_shape, (mega, mega))(parts)
        sums, loss = lax.optimization_barrier((sums, loss))
    with jax.named_scope("loss_far"):
        loss = over_tp(over_tp(loss, 1), tp_count - 2)
    with jax.named_scope("maps_back"):
        grad_q, grad_k = call(
            finish_kernel,
            (shape(heads, half, width), shape(half, width)),
            (mega, mega),
            (STEPS,),
            [whole(*maps_shape.shape)],
            [by_head, whole(half, width)],
        )(exchange_maps(sums))
        grad_q = grad_q.transpose(0, 2, 1)
        grad_k = grad_k.T
        loss = loss[0, 0]
    return grad_q, grad_k[None], loss


def solution(mesh):
    in_specs = (
        P("section", "tp", None),
        P("section", "tp", None),
        P("section", "tp", None),
        P("section", "tp", None),
        P("tp", None, None),
        P("tp", None, None),
    )
    out_specs = (P("tp", None, None), P("tp", None, None), P())
    return jax.shard_map(
        on_device, mesh=mesh, in_specs=in_specs, out_specs=out_specs, check_vma=False
    )
```
